256 devices in a mesh: pipe: 8 (over z_lo, core), ep: 32 (over x, y, z_hi).
Axes of the slice: x: 4, y: 4, z: 8 (z_hi: 2, z_lo: 4; z = z_hi * 4 + z_lo), core: 2. Of those that a mesh axis runs over, the one named last changes fastest.
Arguments:
- x_fwd: bfloat16 [8, 2048, 2048], P('pipe', 'ep'), may hold values from -6 to 6
- ids_fwd: int32 [8, 2048, 8], P('pipe', 'ep'), may hold values from 0 to 31, all different within a row; in each aligned block of 64 rows (0 to 63, 64 to 127, ..., all dimensions but the last counted through in order) at most 24 rows name the same one
- route_fwd: float32 [8, 2048, 8], P('pipe', 'ep'), may hold values from 0.05 to 1
- x_bwd: bfloat16 [8, 2048, 2048], P('pipe', 'ep'), may hold values from -6 to 6
- grad_bwd: bfloat16 [8, 2048, 2048], P('pipe', 'ep'), may hold values from -6 to 6
- ids_bwd: int32 [8, 2048, 8], P('pipe', 'ep'), may hold values from 0 to 31, all different within a row; in each aligned block of 64 rows (0 to 63, 64 to 127, ..., all dimensions but the last counted through in order) at most 24 rows name the same one
- route_bwd: float32 [8, 2048, 8], P('pipe', 'ep'), may hold values from 0.05 to 1
- norm_gain: bfloat16 [8, 2048], P('pipe'), may hold values from 0.25 to 1.75
- w_gate: bfloat16 [8, 32, 2048, 768], P('pipe', 'ep'), may hold values from -0.125 to 0.125
- w_up: bfloat16 [8, 32, 2048, 768], P('pipe', 'ep'), may hold values from -0.125 to 0.125
- w_down: bfloat16 [8, 32, 768, 2048], P('pipe', 'ep'), may hold values from -0.21875 to 0.21875
Outputs:
- fwd_next: bfloat16 [8, 2048, 2048], P('pipe', 'ep')
- bwd_prev: bfloat16 [8, 2048, 2048], P('pipe', 'ep')
The draws below stay inside these ranges and needn't reach their ends.
Inputs may be any that keep to these rules, and one draw needn't show every extreme that they name: `ids_fwd`: in each aligned block of 64 tokens of a section, each token names 8 different experts, no expert is named by more than 24 tokens, and in some block one expert is named by exactly 24. `ids_bwd`: as for ids_fwd.
All inputs are finite; a program needn't handle non-finite values.
Results may differ from the reference program's by a relative error of at most 0.0046.
Values may be sent and summed in bfloat16 or wider, within the bound.
A program may use at most 128 MiB of HBM per device.

```python
import math
import jax
import jax.numpy as jnp
import numpy as np
from jax import lax

D = 2048
FF = 768
TOP = 8
TOK_DEV = 64
SECTIONS = 8
EXPERTS = 32
TOKENS = 2048
CAP = 24
N_EP = 32


def block_scale(stream_key, extent, shards, least, high):
    factor_of = 1.0
    for dim, blocks in shards:
        draws = jax.random.uniform(jax.random.fold_in(jax.random.fold_in(stream_key, 6), dim), (blocks,), jnp.float32, least / len(shards), high / len(shards))
        factor_of = factor_of * jnp.repeat(jnp.exp(draws), extent[dim] // blocks).reshape((-1,) + (1,) * (len(extent) - 1 - dim))
    return factor_of


def shared_out(own_key, own, number, rows, count, top, reach, skew):
    order = jax.random.permutation(own_key, count)
    crowded, usual = shares(count, rows * top, reach, skew, True), shares(count, rows * top, reach, skew, False)
    places = jnp.arange(count)

    def named(tallies, turn):
        used = int((tallies > 0).sum())
        fixed = max(1, used // 4)
        shifted = fixed + (places - fixed + turn * (used - fixed)) % max(1, count - fixed)
        return jnp.zeros((count,), jnp.int32).at[order[jnp.where(places < fixed, places, shifted)]].set(jnp.asarray(tallies, jnp.int32))

    tallies = jnp.where(number % 4 == 0, named(crowded, number // 4), named(usual, number - number // 4 - 1))
    mixed = jax.random.permutation(jax.random.fold_in(own, 3), count)
    donor, receiver = mixed[0:count // 2 * 2:2], mixed[1:count // 2 * 2:2]
    margin = jnp.minimum(tallies[donor] - 1, reach - tallies[receiver]) // 2
    margin = jnp.where((donor == order[0]) | (receiver == order[0]) | (tallies[receiver] == 0), 0, jnp.maximum(margin, 0))
    shifted = jax.random.randint(jax.random.fold_in(own, 4), (count // 2,), 0, 1 << 20) % (margin + 1)
    tallies = tallies.at[donor].add(-shifted).at[receiver].add(shifted)
    members = jnp.searchsorted(jnp.cumsum(tallies), jnp.arange(rows * top), side="right").astype(jnp.int32)
    grid = members.reshape(top, rows).T
    grid = grid[jax.random.permutation(jax.random.fold_in(own, 1), rows)]
    turn = jax.random.randint(jax.random.fold_in(own, 2), (rows, 1), 0, top)
    return jnp.take_along_axis(grid, (jnp.arange(top)[None, :] + turn) % top, axis=1)


def shares(amount, total, reach, skew, full):
    weights = [(1 << 20) // math.isqrt(standing ** skew) + 1 for standing in range(1, amount + 1)]
    largest = reach if full else min(reach, max(-(-total // amount), total * weights[0] // sum(weights)))
    least = 1 if total - largest >= amount - 1 else 0
    given, surplus = [largest] + [least] * (amount - 1), total - largest - least * (amount - 1)
    while surplus > 0:
        movable = [i for i in range(1, amount) if given[i] < largest] or [i for i in range(1, amount) if given[i] < reach]
        whole, budget = sum([weights[i] for i in movable]), surplus
        for i in movable:
            addition = min(reach - given[i], max(1, budget * weights[i] // whole), surplus)
            given[i] = given[i] + addition
            surplus = surplus - addition
    return np.array(given)


def noise(rng, dims, scale, limit, shards=(), kind=jnp.bfloat16):
    values = scale * jax.random.normal(rng, dims, jnp.float32)
    if shards:
        values = values * block_scale(rng, dims, shards, -0.22, 0.18)
    return jnp.clip(values, -limit, limit).astype(kind)


def setup_inputs(seed: int = 0) -> dict:
    arg_keys = jax.random.split(jax.random.key(seed), 12)
    x_fwd = noise(arg_keys[0], (SECTIONS, TOKENS, D), 1.0, 6.0, ((0, 8), (1, 32)))
    ids_fwd_keys = jax.random.split(jax.random.fold_in(arg_keys[1], 1), SECTIONS * TOKENS // TOK_DEV)
    ids_fwd_turns = jax.random.permutation(jax.random.fold_in(arg_keys[1], 3), SECTIONS * TOKENS // TOK_DEV)
    ids_fwd = jax.vmap(lambda own, number: shared_out(jax.random.fold_in(arg_keys[1], 2), own, number, TOK_DEV, EXPERTS, TOP, CAP, 2))(ids_fwd_keys, ids_fwd_turns).reshape((SECTIONS, TOKENS, TOP))
    route_fwd = jnp.clip(jnp.exp(math.log(1.0) - 2.9957323 * jax.random.uniform(arg_keys[2], (SECTIONS, TOKENS, TOP), jnp.float32) ** block_scale(arg_keys[2], (SECTIONS, TOKENS, TOP), ((0, 8), (1, 32)), -0.2, 0.2)), 0.05, 1.0)
    x_bwd = noise(arg_keys[3], (SECTIONS, TOKENS, D), 1.0, 6.0, ((0, 8), (1, 32)))
    grad_bwd = noise(arg_keys[4], (SECTIONS, TOKENS, D), 1.0, 6.0, ((0, 8), (1, 32)))
    ids_bwd_keys = jax.random.split(jax.random.fold_in(arg_keys[5], 1), SECTIONS * TOKENS // TOK_DEV)
    ids_bwd_turns = jax.random.permutation(jax.random.fold_in(arg_keys[5], 3), SECTIONS * TOKENS // TOK_DEV)
    ids_bwd = jax.vmap(lambda own, number: shared_out(jax.random.fold_in(arg_keys[5], 2), own, number, TOK_DEV, EXPERTS, TOP, CAP, 2))(ids_bwd_keys, ids_bwd_turns).reshape((SECTIONS, TOKENS, TOP))
    route_bwd = jnp.clip(jnp.exp(math.log(1.0) - 2.9957323 * jax.random.uniform(arg_keys[6], (SECTIONS, TOKENS, TOP), jnp.float32) ** block_scale(arg_keys[6], (SECTIONS, TOKENS, TOP), ((0, 8), (1, 32)), -0.2, 0.2)), 0.05, 1.0)
    norm_gain = jnp.clip(1.0 + 0.15 * jax.random.normal(arg_keys[7], (SECTIONS, D), jnp.float32), 0.25, 1.75).astype(jnp.bfloat16)
    w_gate = noise(arg_keys[8], (SECTIONS, EXPERTS, D, FF), D ** -0.5, 0.125, ((0, 8), (1, 32)))
    w_up = noise(arg_keys[9], (SECTIONS, EXPERTS, D, FF), D ** -0.5, 0.125, ((0, 8), (1, 32)))
    w_down = noise(arg_keys[10], (SECTIONS, EXPERTS, FF, D), FF ** -0.5, 0.21875, ((0, 8), (1, 32)))
    return dict(x_fwd=x_fwd, ids_fwd=ids_fwd, route_fwd=route_fwd, x_bwd=x_bwd, grad_bwd=grad_bwd, ids_bwd=ids_bwd, route_bwd=route_bwd, norm_gain=norm_gain, w_gate=w_gate, w_up=w_up, w_down=w_down)


EPS = 1e-06

def slot_places(ids, n_exp, cap):
    flat = ids.reshape(-1).astype(jnp.int32)
    onehot = (flat[:, None] == jnp.arange(n_exp, dtype=jnp.int32)[None, :]).astype(jnp.int32)
    before = (jnp.cumsum(onehot, axis=0) - onehot).astype(jnp.int32)
    slot = lax.optimization_barrier(jnp.sum(before * onehot, axis=1)).astype(jnp.int32)
    return (flat * cap + slot).astype(jnp.int32)

def rms_stats(x):
    xf = x.astype(jnp.float32)
    scale = lax.rsqrt(lax.optimization_barrier(jnp.mean(xf * xf, axis=-1, keepdims=True)) + EPS)
    return (xf, scale)

def expert_forward(rows, w_g, w_u, w_d):
    gate = jnp.dot(rows, w_g, preferred_element_type=jnp.float32)
    upper = jnp.dot(rows, w_u, preferred_element_type=jnp.float32)
    act = (jax.nn.silu(gate) * upper).astype(jnp.bfloat16)
    return jnp.dot(act, w_d, preferred_element_type=jnp.float32).astype(jnp.bfloat16)

def expert_backward(rows, cot, w_g, w_u, w_d):
    gate = jnp.dot(rows, w_g, preferred_element_type=jnp.float32)
    upper = jnp.dot(rows, w_u, preferred_element_type=jnp.float32)
    sigma = jax.nn.sigmoid(gate)
    dact = jnp.dot(cot, w_d.T, preferred_element_type=jnp.float32)
    dgate = (dact * upper * sigma * (1.0 + gate * (1.0 - sigma))).astype(jnp.bfloat16)
    dup = (dact * gate * sigma).astype(jnp.bfloat16)
    total = jnp.dot(dgate, w_g.T, preferred_element_type=jnp.float32) + jnp.dot(dup, w_u.T, preferred_element_type=jnp.float32)
    return total.astype(jnp.bfloat16)

def norm_backward(xf, scale, gain, upstream):
    scaled = gain * upstream
    inner = lax.optimization_barrier(jnp.mean(xf * scaled, axis=-1, keepdims=True))
    return scale * scaled - xf * (scale * scale * scale) * inner

def block_places(block):
    return slot_places(block, EXPERTS, CAP)

def tables(ids, route):
    weights = route / lax.optimization_barrier(jnp.sum(route, axis=-1, keepdims=True))
    blocks = ids.reshape(N_EP, TOK_DEV, TOP).astype(jnp.int32)
    places = jax.vmap(block_places)(blocks)
    flat_e = blocks.reshape(N_EP, TOK_DEV * TOP)
    slot = (places - flat_e * CAP).astype(jnp.int32)
    source = jnp.arange(N_EP, dtype=jnp.int32)[:, None]
    column = (source * CAP + slot).astype(jnp.int32)
    token = (source * TOK_DEV + jnp.arange(TOK_DEV * TOP, dtype=jnp.int32)[None, :] // TOP).astype(jnp.int32)
    table = jnp.full((EXPERTS, N_EP * CAP), -1, jnp.int32).at[flat_e, column].set(token)
    wtable = jnp.zeros((EXPERTS, N_EP * CAP), jnp.float32).at[flat_e, column].set(weights.reshape(N_EP, TOK_DEV * TOP))
    return (table, wtable)

def section(operands):
    x_f, ids_f, route_f, x_b, grad_b, ids_b, route_b, gain, w_g, w_u, w_d = operands
    gainf = gain.astype(jnp.float32)
    xf, scale_f = rms_stats(x_f)
    h_f = (xf * scale_f * gainf).astype(jnp.bfloat16)
    xb, scale_b = rms_stats(x_b)
    h_b = (xb * scale_b * gainf).astype(jnp.bfloat16)
    table_f, wtable_f = tables(ids_f, route_f)
    table_b, wtable_b = tables(ids_b, route_b)
    zero_b = jnp.zeros((), jnp.bfloat16)

    def per_expert(carry, expert):
        out_f, out_b = carry
        index = table_f[expert]
        valid = (index >= 0)[:, None]
        safe = jnp.maximum(index, 0)
        rows = jnp.where(valid, h_f[safe], zero_b)
        outcome = expert_forward(rows, w_g[expert], w_u[expert], w_d[expert])
        out_f = out_f.at[safe].add(jnp.where(valid, wtable_f[expert][:, None] * outcome.astype(jnp.float32), 0.0))
        index = table_b[expert]
        valid = (index >= 0)[:, None]
        safe = jnp.maximum(index, 0)
        rows = jnp.where(valid, h_b[safe], zero_b)
        cot = jnp.where(valid, (wtable_b[expert][:, None] * grad_b[safe].astype(jnp.float32)).astype(jnp.bfloat16), zero_b)
        back = expert_backward(rows, cot, w_g[expert], w_u[expert], w_d[expert])
        out_b = out_b.at[safe].add(jnp.where(valid, back.astype(jnp.float32), 0.0))
        return ((out_f, out_b), None)
    start = (jnp.zeros((TOKENS, D), jnp.float32), jnp.zeros((TOKENS, D), jnp.float32))
    (mixed, dnorm), _ = lax.scan(per_expert, start, jnp.arange(EXPERTS, dtype=jnp.int32))
    y = (xf + mixed).astype(jnp.bfloat16)
    dx = (grad_b.astype(jnp.float32) + norm_backward(xb, scale_b, gainf, dnorm)).astype(jnp.bfloat16)
    return (y, dx)

def reference(x_fwd, ids_fwd, route_fwd, x_bwd, grad_bwd, ids_bwd, route_bwd, norm_gain, w_gate, w_up, w_down):
    y, dx = lax.map(section, (x_fwd, ids_fwd, route_fwd, x_bwd, grad_bwd, ids_bwd, route_bwd, norm_gain, w_gate, w_up, w_down))
    return (jnp.roll(y, 1, axis=0), jnp.roll(dx, -1, axis=0))
```

```python
import functools

import jax
import jax.numpy as jnp
from jax import lax
from jax.experimental import pallas as pl
from jax.experimental.pallas import tpu as pltpu
from jax.sharding import PartitionSpec as P

EPS = 1e-06
MESH = pl.DeviceIdType.MESH
F32, BF16 = jnp.float32, jnp.bfloat16

SIDE = 4
TOK = 64
CAP = 24
PAIR = 2 * CAP
D = 2048
HALF = D // 2
FF = 768
TOP = 8
NT = 256
G, HB, HF = 0, 1, 2
FWD, BWD = 0, 1


def dot(a, b):
    return jnp.dot(a, b, preferred_element_type=F32)


def dot_t(a, b):
    return lax.dot_general(a, b, (((1,), (1,)), ((), ())), preferred_element_type=F32)


def kernel(
    xf_ref, idf_ref, rtf_ref, xb_ref, gr_ref, idb_ref, rtb_ref, gain_ref, wg_hbm, wu_hbm, wd_hbm,
    outf_ref, outb_ref,
    wg, wu, wd, dense, pool, slots, ret, part, own, gath, zout, zin, last, act1, act2,
    meta, meta_z, meta_d, sel, sel_t, slot_w,
    w_sem, mz_s, mz_r, ma_s, ma_r, zs, zr, ds_s, ds_r, xs, xr, rs, rr, cs, cr, qs, qr, ps, pr,
):
    p = lax.axis_index("pipe")
    e = lax.axis_index("ep")
    x, y, z = e // 8, lax.rem(e // 2, SIDE), lax.rem(e, 2)

    def at(dx, dy, dz):
        return (p, lax.rem(x + dx, SIDE) * 8 + lax.rem(y + dy, SIDE) * 2 + lax.rem(z + dz, 2))

    def first(q, d):
        return at(0, d, 0) if q == 0 else at(d, 0, 0)

    def second(q, d):
        return first(1 - q, d)

    partner = at(0, 0, 1)
    ahead, behind = (lax.rem(p + 1, 8), e), (lax.rem(p + 7, 8), e)

    def send(src, dst, s, r, device):
        pltpu.make_async_remote_copy(
            src_ref=src, dst_ref=dst, send_sem=s, recv_sem=r, device_id=device, device_id_type=MESH
        ).start()

    def take(ref, sem):
        pltpu.make_async_copy(ref, ref, sem).wait()

    barrier = pltpu.get_barrier_semaphore()
    for device in [partner, ahead, behind] + [first(q, d) for q in (0, 1) for d in (1, 2, 3)]:
        pl.semaphore_signal(barrier, inc=1, device_id=device, device_id_type=MESH)
    loads = [
        pltpu.make_async_copy(src, dst, w_sem.at[i])
        for i, (src, dst) in enumerate(((wg_hbm, wg), (wu_hbm, wu), (wd_hbm, wd)))
    ]
    for load in loads:
        load.start()

    shape = (2 * TOK, 128)
    row = lax.broadcasted_iota(jnp.int32, shape, 1)
    i, d, q, dz = row % 4, (row // 8) % 4, (row // 32) % 2, row // 64
    ex = jnp.where(q == 0, i, d)
    ey = jnp.where(q == 0, d, i)
    expert = ((x + ex) % SIDE) * 8 + ((y + ey) % SIDE) * 2 + (z + dz) % 2
    ids = jnp.concatenate([idf_ref[...], idb_ref[...]], axis=0)
    route = jnp.concatenate([rtf_ref[...], rtb_ref[...]], axis=0)
    route = route / jnp.sum(route, axis=-1, keepdims=True)
    picked = jnp.zeros(shape, F32)
    weight = jnp.zeros(shape, F32)
    for k in range(TOP):
        hit = ids[:, k : k + 1] == expert
        picked = jnp.where(hit, 1.0, picked)
        weight = jnp.where(hit, route[:, k : k + 1], weight)
    picked, weight = picked.T, weight.T
    early = lax.broadcasted_iota(jnp.int32, (128, 128), 0)
    late = lax.broadcasted_iota(jnp.int32, (128, 128), 1)
    order = jnp.where((early < late) & (early // TOK == late // TOK), 1.0, 0.0).astype(BF16)
    before = dot(picked.astype(BF16), order)
    place = jnp.where(picked > 0.0, before, -1000.0)
    kind = (lax.broadcasted_iota(jnp.int32, (128, 128), 0) // 4) % 2
    meta[...] = jnp.where(kind == 0, place, weight).reshape(2, 2, 4, 8, 128)
    pl.semaphore_wait(barrier, 9)

    def send_own(t):
        for q in (0, 1):
            send(dense.at[t, q, 0, 0], dense.at[t, q, 0, 1], zs.at[t, q], zr.at[t, q], partner)
        for q in (0, 1):
            for d in (2, 1, 3):
                there = dense.at[t, q, SIDE - d, 0]
                send(dense.at[t, q, 0, 0], there, ds_s.at[t], ds_r.at[t, q, SIDE - d, 0], first(q, d))

    def send_partners(t):
        for q in (0, 1):
            take(dense.at[t, q, 0, 1], zr.at[t, q])
            for d in (2, 1, 3):
                there = dense.at[t, q, SIDE - d, 1]
                send(dense.at[t, q, 0, 1], there, ds_s.at[t], ds_r.at[t, q, SIDE - d, 1], first(q, d))

    def normed(ref, t):
        v = ref[...].astype(F32)
        scale = lax.rsqrt(jnp.mean(v * v, axis=-1, keepdims=True) + EPS)
        h = (v * scale * gain_ref[...].astype(F32)).astype(BF16)
        for q in (0, 1):
            dense[t, q, 0, 0] = h[:, q * HALF : (q + 1) * HALF]

    send(meta.at[1], meta_z, mz_s, mz_r, partner)
    for q in (0, 1):
        for d in (1, 2, 3):
            send(meta.at[0, q, d], meta_d.at[q, SIDE - d, 0], ma_s, ma_r, first(q, d))
        dense[G, q, 0, 0] = gr_ref[:, q * HALF : (q + 1) * HALF]
    send_own(G)
    normed(xb_ref, HB)
    send_own(HB)
    take(meta_z, mz_r)
    for q in (0, 1):
        for d in (1, 2, 3):
            send(meta_z.at[q, d], meta_d.at[q, SIDE - d, 1], ma_s, ma_r, first(q, d))
        meta_d[q, 0, 0] = meta[0, q, 0]
        meta_d[q, 0, 1] = meta_z[q, 0]
    normed(xf_ref, HF)
    take(meta_d.at[:, 1:4], ma_r)

    lane = lax.broadcasted_iota(jnp.int32, (8, 128), 1)
    slot = lax.broadcasted_iota(jnp.int32, (PAIR, 128), 0).astype(F32)

    @pl.loop(0, 8)
    def _(n):
        q, d = n // 4, lax.rem(n, 4)
        m0, m1 = meta_d[q, d, 0], meta_d[q, d, 1]
        r0, r1 = pltpu.roll(m0, TOK, 1), pltpu.roll(m1, TOK, 1)
        for way, m in ((FWD, jnp.where(lane < TOK, m0, r1)), (BWD, jnp.where(lane < TOK, r0, m1))):
            shifted = m + jnp.where(lane < TOK, 0.0, 1.0 * CAP)
            ones, weighed = [], []
            for i in range(SIDE):
                hit = jnp.broadcast_to(shifted[i : i + 1], (PAIR, 128)) == slot
                ones.append(jnp.where(hit, 1.0, 0.0))
                weighed.append(jnp.where(hit, jnp.broadcast_to(m[4 + i : 5 + i], (PAIR, 128)), 0.0))
            fill = [jnp.zeros((256 - SIDE * PAIR, 128), F32)]
            one = jnp.concatenate(ones, axis=0)
            w = jnp.concatenate(weighed, axis=0)
            sel[way, q, d] = one.astype(BF16)
            if way == BWD:
                sum_w = jnp.sum(w, axis=1, keepdims=True)
                slot_w[q, d] = jnp.broadcast_to(sum_w, (SIDE * PAIR, 128))
                back = jnp.concatenate([one] + fill, axis=0).T
                sel_t[2, q, d] = back[:, : SIDE * PAIR].astype(BF16)
            else:
                back = jnp.concatenate([w] + fill, axis=0).T[:, : SIDE * PAIR]
                high = back.astype(BF16)
                sel_t[0, q, d] = high
                sel_t[1, q, d] = (back - high.astype(F32)).astype(BF16)

    def block(ref, q, a, b):
        return ref.at[a, b] if q == 1 else ref.at[b, a]

    def send_slots(t, q, d):
        way = FWD if t == HF else BWD
        for n in range(HALF // NT):
            cols = slice(n * NT, (n + 1) * NT)
            rows = dot(sel[way, q, d], dense[t, q, d, :, :, cols].reshape(2 * TOK, NT))
            if t == G:
                rows = rows * jnp.concatenate([slot_w[q, d]] * (NT // 128), axis=1)
            rows = rows.astype(BF16)
            block(slots.at[t, q], q, d, 0)[:, cols] = rows[:PAIR]
            pool[t, q, d, :, :, cols] = rows[PAIR:].reshape(SIDE - 1, PAIR, NT)
        for i in (2, 1, 3):
            there = block(slots.at[t, q], q, d, SIDE - i)
            send(pool.at[t, q, d, i - 1], there, xs.at[t], xr.at[t, q], second(q, i))

    def send_other_slots(t):
        @pl.loop(1, SIDE)
        def _(d):
            for q in (0, 1):
                for dz in (0, 1):
                    take(dense.at[t, q, d, dz], ds_r.at[t, q, d, dz])
                send_slots(t, q, d)

    send_partners(G)
    for q in (0, 1):
        send_slots(G, q, 0)
    send_own(HF)
    send_other_slots(G)
    send_partners(HB)
    for q in (0, 1):
        send_slots(HB, q, 0)
    send_other_slots(HB)
    send_partners(HF)
    for q in (0, 1):
        send_slots(HF, q, 0)
    send_other_slots(HF)

    for load in loads:
        load.wait()

    def arrived(t):
        for q in (0, 1):
            take(slots.at[t, q, 0:3], xr.at[t, q])

    def rows_of(t, q, h):
        return slots[t, q, pl.ds(2 * h, 2)].reshape(2 * SIDE * PAIR, HALF)

    def gate_up(t, h, n):
        cols = pl.ds(pl.multiple_of(n * NT, NT), NT)
        r0, r1 = rows_of(t, 0, h), rows_of(t, 1, h)
        a = dot(r0, wg[:HALF, cols]) + dot(r1, wg[HALF:, cols])
        u = dot(r0, wu[:HALF, cols]) + dot(r1, wu[HALF:, cols])
        return a, u, cols

    n_rows = 2 * SIDE * PAIR

    def send_back(way, make):
        for step in range(4):
            q, h = step % 2, 1 - step // 2

            @pl.loop(0, HALF // NT)
            def _(n, q=q, h=h):
                cols = pl.ds(pl.multiple_of(n * NT, NT), NT)
                made = make(q, h, n).astype(BF16)
                for k in range(2 * SIDE):
                    dx, dy = 2 * h + k // SIDE, k % SIDE
                    b, a = (dx, dy) if q == 0 else (dy, dx)
                    one = made[k * PAIR : (k + 1) * PAIR]
                    if b == 0:
                        ret[way, q, a, 0, :, cols] = one
                    else:
                        pool[way, q, a, b - 1, :, cols] = one

            for k in range(2 * SIDE):
                dx, dy = 2 * h + k // SIDE, k % SIDE
                b, a = (dx, dy) if q == 0 else (dy, dx)
                if b:
                    there = ret.at[way, q, a, SIDE - b]
                    send(pool.at[way, q, a, b - 1], there, rs.at[way], rr.at[way, q, a], second(q, b))

    arrived(G)
    arrived(HB)

    @pl.loop(0, 6)
    def _(step):
        h, n = step // 3, lax.rem(step, 3)
        a, u, cols = gate_up(HB, h, n)
        r0, r1 = rows_of(G, 0, h), rows_of(G, 1, h)
        dact = dot_t(r0, wd[cols, :HALF]) + dot_t(r1, wd[cols, HALF:])
        sg = jax.nn.sigmoid(a)
        rows = pl.ds(pl.multiple_of(h * n_rows, n_rows), n_rows)
        act1[rows, cols] = (dact * u * sg * (1.0 + a * (1.0 - sg))).astype(BF16)
        act2[rows, cols] = (dact * a * sg).astype(BF16)

    for t in (G, HB):
        take(pool.at[t], xs.at[t])

    def make_dh(q, h, n):
        rows = pl.ds(pl.multiple_of(q * HALF + n * NT, NT), NT)
        mine = slice(h * n_rows, (h + 1) * n_rows)
        return dot_t(act1[mine], wg[rows]) + dot_t(act2[mine], wu[rows])

    send_back(BWD, make_dh)
    arrived(HF)

    @pl.loop(0, 6)
    def _(step):
        h, n = step // 3, lax.rem(step, 3)
        a, u, cols = gate_up(HF, h, n)
        rows = pl.ds(pl.multiple_of(h * n_rows, n_rows), n_rows)
        act1[rows, cols] = (a * jax.nn.sigmoid(a) * u).astype(BF16)

    def make_o(q, h, n):
        cols = pl.ds(pl.multiple_of(q * HALF + n * NT, NT), NT)
        return dot(act1[h * n_rows : (h + 1) * n_rows], wd[:, cols])

    send_back(FWD, make_o)

    def combine(way, q, d):
        take(ret.at[way, q, d, 0:3], rr.at[way, q, d])
        for n in range(HALF // NT):
            cols = slice(n * NT, (n + 1) * NT)
            rows = ret[way, q, d, :, :, cols].reshape(SIDE * PAIR, NT)
            if way == BWD:
                total = dot(sel_t[2, q, d], rows)
            else:
                total = dot(sel_t[0, q, d], rows) + dot(sel_t[1, q, d], rows)
            if d == 0:
                own[q, :, cols] = total
            else:
                part[way, q, d - 1, :, cols] = total.astype(BF16)
        if d:
            there = gath.at[way, q, SIDE - d - 1]
            send(part.at[way, q, d - 1], there, cs.at[way], cr.at[way, q], first(q, d))

    def cross(way, q):
        take(gath.at[way, q], cr.at[way, q])
        total = own[q]
        for d in range(SIDE - 1):
            total = total + gath[way, q, d].astype(F32)
        zout[way, q] = total[TOK:].astype(BF16)
        send(zout.at[way, q], zin.at[way, q], qs.at[way, q], qr.at[way, q], partner)
        own[q, :TOK] = total[:TOK]

    def mixed(way, q):
        take(zin.at[way, q], qr.at[way, q])
        return own[q, :TOK] + zin[way, q].astype(F32)

    def gather(way):
        for d in (2, 1, 3, 0):
            for q in (0, 1):
                combine(way, q, d)
        for q in (0, 1):
            cross(way, q)

    gather(BWD)
    dn = jnp.concatenate([mixed(BWD, 0), mixed(BWD, 1)], axis=1)
    xb = xb_ref[...].astype(F32)
    scale = lax.rsqrt(jnp.mean(xb * xb, axis=-1, keepdims=True) + EPS)
    v = gain_ref[...].astype(F32) * dn
    inner = jnp.mean(xb * v, axis=-1, keepdims=True)
    dx = scale * v - xb * (scale * scale * scale) * inner
    last[BWD] = (gr_ref[...].astype(F32) + dx).astype(BF16)
    send(last.at[BWD], outb_ref, ps.at[BWD], pr.at[BWD], behind)
    gather(FWD)
    for q in (0, 1):
        cols = slice(q * HALF, (q + 1) * HALF)
        last[FWD, :, cols] = (xf_ref[:, cols].astype(F32) + mixed(FWD, q)).astype(BF16)
    send(last.at[FWD], outf_ref, ps.at[FWD], pr.at[FWD], ahead)

    take(outb_ref, pr.at[BWD])
    take(outf_ref, pr.at[FWD])
    take(meta_z, mz_s)
    take(meta_d.at[:, 1:4], ma_s)
    for t in (G, HB, HF):
        take(dense.at[t, :, 1:4], ds_s.at[t])
        for q in (0, 1):
            take(dense.at[t, q, 0, 0], zs.at[t, q])
    take(pool.at[HF], xs.at[HF])
    for way in (FWD, BWD):
        take(pool.at[way], rs.at[way])
        take(part.at[way], cs.at[way])
        for q in (0, 1):
            take(zout.at[way, q], qs.at[way, q])
        take(last.at[way], ps.at[way])


def local(*args):
    args = [a.reshape(a.shape[-2:]) for a in args]
    vm = pl.BlockSpec(memory_space=pltpu.VMEM)
    hbm = pl.BlockSpec(memory_space=pl.ANY)
    dma = pltpu.SemaphoreType.DMA
    out = jax.ShapeDtypeStruct((TOK, D), BF16)
    slots = (SIDE - 1, PAIR, HALF)
    got = pl.pallas_call(
        kernel,
        name="expert_layer",
        out_shape=(out, out),
        in_specs=[vm] * 8 + [hbm] * 3,
        out_specs=(vm, vm),
        scratch_shapes=[
            pltpu.VMEM((D, FF), BF16),
            pltpu.VMEM((D, FF), BF16),
            pltpu.VMEM((FF, D), BF16),
            pltpu.VMEM((3, 2, SIDE, 2, TOK, HALF), BF16),
            pltpu.VMEM((3, 2, SIDE) + slots, BF16),
            pltpu.VMEM((3, 2, SIDE, SIDE, PAIR, HALF), BF16),
            pltpu.VMEM((2, 2, SIDE, SIDE, PAIR, HALF), BF16),
            pltpu.VMEM((2, 2, SIDE - 1, 2 * TOK, HALF), BF16),
            pltpu.VMEM((2, 2 * TOK, HALF), F32),
            pltpu.VMEM((2, 2, SIDE - 1, 2 * TOK, HALF), BF16),
            pltpu.VMEM((2, 2, TOK, HALF), BF16),
            pltpu.VMEM((2, 2, TOK, HALF), BF16),
            pltpu.VMEM((2, TOK, D), BF16),
            pltpu.VMEM((SIDE * SIDE * PAIR, FF), BF16),
            pltpu.VMEM((SIDE * SIDE * PAIR, FF), BF16),
            pltpu.VMEM((2, 2, SIDE, 8, 128), F32),
            pltpu.VMEM((2, SIDE, 8, 128), F32),
            pltpu.VMEM((2, SIDE, 2, 8, 128), F32),
            pltpu.VMEM((2, 2, SIDE, SIDE * PAIR, 2 * TOK), BF16),
            pltpu.VMEM((3, 2, SIDE, 2 * TOK, SIDE * PAIR), BF16),
            pltpu.VMEM((2, SIDE, SIDE * PAIR, 128), F32),
            dma((3,)),
            dma,
            dma,
            dma,
            dma,
            dma((3, 2)),
            dma((3, 2)),
            dma((3,)),
            dma((3, 2, SIDE, 2)),
            dma((3,)),
            dma((3, 2)),
            dma((2,)),
            dma((2, 2, SIDE)),
            dma((2,)),
            dma((2, 2)),
            dma((2, 2)),
            dma((2, 2)),
            dma((2,)),
            dma((2,)),
        ],
        compiler_params=pltpu.CompilerParams(
            collective_id=0, has_side_effects=True, vmem_limit_bytes=62 * 1024 * 1000
        ),
        cost_estimate=pl.CostEstimate(
            flops=2 * 8 * 768 * D * FF, bytes_accessed=3 * 2 * D * FF, transcendentals=2 * 768 * FF
        ),
    )(*args)
    return tuple(o[None] for o in got)


def solution(mesh):
    rows = P("pipe", "ep", None)
    weights = P("pipe", "ep", None, None)
    return jax.shard_map(
        local,
        mesh=mesh,
        in_specs=(rows,) * 7 + (P("pipe", None),) + (weights,) * 3,
        out_specs=(rows, rows),
        check_vma=False,
    )
```

```python
import functools

import jax
import jax.numpy as jnp
from jax import lax
from jax.experimental import pallas as pl
from jax.experimental.pallas import tpu as pltpu
from jax.sharding import PartitionSpec as P

EPS = 1e-06
MESH = pl.DeviceIdType.MESH
F32, BF16 = jnp.float32, jnp.bfloat16

SIDE = 4
TOK = 64
CAP = 24
PAIR = 2 * CAP
D = 2048
HALF = D // 2
CHUNKS = 4
WIDE = HALF // CHUNKS
FF = 768
TOP = 8
NT = 256
G, HB, HF = 0, 1, 2
FWD, BWD = 0, 1


def dot(a, b):
    return jnp.dot(a, b, preferred_element_type=F32)


def dot_t(a, b):
    return lax.dot_general(a, b, (((1,), (1,)), ((), ())), preferred_element_type=F32)


def kernel(
    xf_ref, idf_ref, rtf_ref, xb_ref, gr_ref, idb_ref, rtb_ref, gain_ref, wg_hbm, wu_hbm, wd_hbm,
    outf_ref, outb_ref,
    wg, wu, wd, dense, pool, slots, ret, part, own, gath, zout, zin, last, act1, act2,
    meta, meta_z, meta_d, sel, sel_t, slot_w,
    w_sem, mz_s, mz_r, ma_s, ma_r, zs, zr, ds_s, ds_r, xs, xr, rs, rr, cs, cr, qs, qr, ps, pr,
):
    p = lax.axis_index("pipe")
    e = lax.axis_index("ep")
    x, y, z = e // 8, lax.rem(e // 2, SIDE), lax.rem(e, 2)

    def at(dx, dy, dz):
        return (p, lax.rem(x + dx, SIDE) * 8 + lax.rem(y + dy, SIDE) * 2 + lax.rem(z + dz, 2))

    def first(q, d):
        return at(0, d, 0) if q == 0 else at(d, 0, 0)

    def second(q, d):
        return first(1 - q, d)

    partner = at(0, 0, 1)
    ahead, behind = (lax.rem(p + 1, 8), e), (lax.rem(p + 7, 8), e)

    def send(src, dst, s, r, device):
        pltpu.make_async_remote_copy(
            src_ref=src, dst_ref=dst, send_sem=s, recv_sem=r, device_id=device, device_id_type=MESH
        ).start()

    def take(ref, sem):
        pltpu.make_async_copy(ref, ref, sem).wait()

    barrier = pltpu.get_barrier_semaphore()
    for device in [partner, ahead, behind] + [first(q, d) for q in (0, 1) for d in (1, 2, 3)]:
        pl.semaphore_signal(barrier, inc=1, device_id=device, device_id_type=MESH)
    loads = [
        pltpu.make_async_copy(src, dst, w_sem.at[i])
        for i, (src, dst) in enumerate(((wg_hbm, wg), (wu_hbm, wu), (wd_hbm, wd)))
    ]
    for load in loads:
        load.start()

    def send_across(t, q):
        send(dense.at[t, q, 0, 0], dense.at[t, q, 0, 1], zs.at[t, q], zr.at[t, q], partner)

    def to_first(t, q, d, dz, to):
        there = dense.at[t, q, (d - to) % SIDE, dz]
        send(dense.at[t, q, d, dz], there, ds_s.at[t], ds_r.at[t, q, (d - to) % SIDE, dz], first(q, to))

    def send_own(t):
        for to in (1, 3):
            for q in (0, 1):
                to_first(t, q, 0, 0, to)

    def forward_own(t):
        for q in (0, 1):
            take(dense.at[t, q, 3, 0], ds_r.at[t, q, 3, 0])
            to_first(t, q, 3, 0, 1)

    def normed(ref, t):
        v = ref[...].astype(F32)
        scale = lax.rsqrt(jnp.mean(v * v, axis=-1, keepdims=True) + EPS)
        h = (v * scale * gain_ref[...].astype(F32)).astype(BF16)
        for q in (0, 1):
            dense[t, q, 0, 0] = h[:, q * HALF : (q + 1) * HALF]

    row = lax.broadcasted_iota(jnp.int32, (128, 128), 0)
    i, d, q, dz = row % 4, (row // 8) % 4, (row // 32) % 2, row // 64
    ex = jnp.where(q == 0, i, d)
    ey = jnp.where(q == 0, d, i)
    expert = ((x + ex) % SIDE) * 8 + ((y + ey) % SIDE) * 2 + (z + dz) % 2
    ids = jnp.concatenate([idf_ref[...], idb_ref[...]], axis=1)
    route = jnp.concatenate([rtf_ref[...], rtb_ref[...]], axis=1)
    route = route / jnp.sum(route, axis=0, keepdims=True)
    picked = jnp.zeros((128, 128), F32)
    weight = jnp.zeros((128, 128), F32)
    for k in range(TOP):
        hit = jnp.broadcast_to(ids[k : k + 1], (128, 128)) == expert
        picked = jnp.where(hit, 1.0, picked)
        weight = jnp.where(hit, jnp.broadcast_to(route[k : k + 1], (128, 128)), weight)
    early = lax.broadcasted_iota(jnp.int32, (128, 128), 0)
    late = lax.broadcasted_iota(jnp.int32, (128, 128), 1)
    order = jnp.where((early < late) & (early // TOK == late // TOK), 1.0, 0.0).astype(BF16)
    before = dot(picked.astype(BF16), order)
    place = jnp.where(picked > 0.0, before, -1000.0)
    kind = (row // 4) % 2
    meta[...] = jnp.where(kind == 0, place, weight).reshape(2, 2, 4, 8, 128)
    for q in (0, 1):
        dense[G, q, 0, 0] = gr_ref[:, q * HALF : (q + 1) * HALF]
    pl.semaphore_wait(barrier, 9)
    send(meta.at[1], meta_z, mz_s, mz_r, partner)
    for q in (0, 1):
        for d in (1, 2, 3):
            send(meta.at[0, q, d], meta_d.at[q, SIDE - d, 0], ma_s, ma_r, first(q, d))
    send_across(G, 0)
    send_across(G, 1)
    send_own(G)
    normed(xb_ref, HB)
    take(meta_z, mz_r)
    for q in (0, 1):
        for d in (1, 2, 3):
            send(meta_z.at[q, d], meta_d.at[q, SIDE - d, 1], ma_s, ma_r, first(q, d))
        meta_d[q, 0, 0] = meta[0, q, 0]
        meta_d[q, 0, 1] = meta_z[q, 0]
    send_across(HB, 0)
    send_across(HB, 1)
    send_own(HB)
    normed(xf_ref, HF)
    send_across(HF, 0)
    send_across(HF, 1)
    send_own(HF)
    forward_own(G)
    take(meta_d.at[:, 1:4], ma_r)

    lane = lax.broadcasted_iota(jnp.int32, (8, 128), 1)
    slot = lax.broadcasted_iota(jnp.int32, (PAIR, 128), 0).astype(F32)

    @pl.loop(0, 8)
    def _(n):
        q, d = n // 4, lax.rem(n, 4)
        m0, m1 = meta_d[q, d, 0], meta_d[q, d, 1]
        r0, r1 = pltpu.roll(m0, TOK, 1), pltpu.roll(m1, TOK, 1)
        for way, m in ((FWD, jnp.where(lane < TOK, m0, r1)), (BWD, jnp.where(lane < TOK, r0, m1))):
            shifted = m + jnp.where(lane < TOK, 0.0, 1.0 * CAP)
            ones, weighed = [], []
            for i in range(SIDE):
                hit = jnp.broadcast_to(shifted[i : i + 1], (PAIR, 128)) == slot
                ones.append(jnp.where(hit, 1.0, 0.0))
                weighed.append(jnp.where(hit, jnp.broadcast_to(m[4 + i : 5 + i], (PAIR, 128)), 0.0))
            fill = [jnp.zeros((256 - SIDE * PAIR, 128), F32)]
            one = jnp.concatenate(ones, axis=0)
            w = jnp.concatenate(weighed, axis=0)
            sel[way, q, d] = one.astype(BF16)
            if way == BWD:
                sum_w = jnp.sum(w, axis=1, keepdims=True)
                slot_w[q, d] = jnp.broadcast_to(sum_w, (SIDE * PAIR, 128))
                back = jnp.concatenate([one] + fill, axis=0).T
                sel_t[2, q, d] = back[:, : SIDE * PAIR].astype(BF16)
            else:
                back = jnp.concatenate([w] + fill, axis=0).T[:, : SIDE * PAIR]
                high = back.astype(BF16)
                sel_t[0, q, d] = high
                sel_t[1, q, d] = (back - high.astype(F32)).astype(BF16)

    def block(ref, q, a, b):
        return ref.at[a, b] if q == 1 else ref.at[b, a]

    def send_slots(t, d):
        way = FWD if t == HF else BWD
        for q in (0, 1):

            @pl.loop(0, HALF // NT)
            def _(n, q=q):
                cols = pl.ds(pl.multiple_of(n * NT, NT), NT)
                rows = dot(sel[way, q, d], dense[t, q, d, :, :, cols].reshape(2 * TOK, NT))
                if t == G:
                    rows = rows * jnp.concatenate([slot_w[q, d]] * (NT // 128), axis=1)
                rows = rows.astype(BF16)
                block(slots.at[t, q], q, d, 0)[:, cols] = rows[:PAIR]
                for k in range(1, SIDE):
                    pool[t, q, k, d, :, cols] = rows[k * PAIR : (k + 1) * PAIR]

        for i in (1, 3, 2):
            for q in (0, 1):
                there = block(slots.at[t, q], q, d, SIDE - i)
                send(pool.at[t, q, i, d], there, xs.at[t], xr.at[t, q], second(q, i))

    def near(t):
        for q in (0, 1):
            take(dense.at[t, q, 0, 1], zr.at[t, q])
            to_first(t, q, 0, 1, 3)
        for q in (0, 1):
            to_first(t, q, 0, 1, 1)
        send_slots(t, 0)

    def far(t):
        for q in (0, 1):
            take(dense.at[t, q, 1, 1], ds_r.at[t, q, 1, 1])
            to_first(t, q, 1, 1, 3)
        for d, news in ((3, (1,)), (1, (0,)), (2, (0, 1))):
            for dz in news:
                for q in (0, 1):
                    take(dense.at[t, q, d, dz], ds_r.at[t, q, d, dz])
            send_slots(t, d)

    near(G)
    forward_own(HB)
    forward_own(HF)
    far(G)
    near(HB)
    far(HB)
    near(HF)
    far(HF)

    for load in loads:
        load.wait()

    def arrived(t):
        for q in (0, 1):
            take(slots.at[t, q, 0:3], xr.at[t, q])

    def rows_of(t, q, h):
        return slots[t, q, pl.ds(2 * h, 2)].reshape(2 * SIDE * PAIR, HALF)

    def gate_up(t, h, n):
        cols = pl.ds(pl.multiple_of(n * NT, NT), NT)
        r0, r1 = rows_of(t, 0, h), rows_of(t, 1, h)
        a = dot(r0, wg[:HALF, cols]) + dot(r1, wg[HALF:, cols])
        u = dot(r0, wu[:HALF, cols]) + dot(r1, wu[HALF:, cols])
        return a, u, cols

    n_rows = 2 * SIDE * PAIR

    def chunk(c):
        return slice(c * WIDE, (c + 1) * WIDE)

    def send_back(way, c, make):
        for q in (0, 1):

            @pl.loop(0, 2 * (WIDE // NT))
            def _(step, q=q):
                h, n = lax.rem(step, 2), step // 2 + c * (WIDE // NT)
                cols = pl.ds(pl.multiple_of(n * NT, NT), NT)
                made = make(q, h, n).astype(BF16)
                for k in range(2 * SIDE):
                    one = made[k * PAIR : (k + 1) * PAIR]
                    if q == 0:
                        pool[way, q, 2 * h + k // SIDE, k % SIDE, :, cols] = one
                    else:
                        pool[way, q, k % SIDE, 2 * h + k // SIDE, :, cols] = one

        for d in range(SIDE):
            for b in (1, 3, 2):
                for q in (0, 1):
                    there = ret.at[way, q, SIDE - b, d, :, chunk(c)]
                    send(pool.at[way, q, b, d, :, chunk(c)], there, rs.at[way, c], rr.at[way, q, c], second(q, b))
        for q in (0, 1):
            ret[way, q, 0, :, :, chunk(c)] = pool[way, q, 0, :, :, chunk(c)]

    arrived(G)
    arrived(HB)

    @pl.loop(0, 6)
    def _(step):
        h, n = step // 3, lax.rem(step, 3)
        a, u, cols = gate_up(HB, h, n)
        r0, r1 = rows_of(G, 0, h), rows_of(G, 1, h)
        dact = dot_t(r0, wd[cols, :HALF]) + dot_t(r1, wd[cols, HALF:])
        sg = jax.nn.sigmoid(a)
        rows = pl.ds(pl.multiple_of(h * n_rows, n_rows), n_rows)
        act1[rows, cols] = (dact * u * sg * (1.0 + a * (1.0 - sg))).astype(BF16)
        act2[rows, cols] = (dact * a * sg).astype(BF16)

    for t in (G, HB):
        take(pool.at[t, :, 1:4], xs.at[t])

    def make_dh(q, h, n):
        rows = pl.ds(pl.multiple_of(q * HALF + n * NT, NT), NT)
        mine = pl.ds(pl.multiple_of(h * n_rows, n_rows), n_rows)
        return dot_t(act1[mine], wg[rows]) + dot_t(act2[mine], wu[rows])

    for c in range(CHUNKS):
        send_back(BWD, c, make_dh)
    arrived(HF)

    @pl.loop(0, 6)
    def _(step):
        h, n = step // 3, lax.rem(step, 3)
        a, u, cols = gate_up(HF, h, n)
        rows = pl.ds(pl.multiple_of(h * n_rows, n_rows), n_rows)
        act1[rows, cols] = (a * jax.nn.sigmoid(a) * u).astype(BF16)

    def make_o(q, h, n):
        cols = pl.ds(pl.multiple_of(q * HALF + n * NT, NT), NT)
        return dot(act1[pl.ds(pl.multiple_of(h * n_rows, n_rows), n_rows)], wd[:, cols])

    def combine(way, c):
        for q in (0, 1):
            take(ret.at[way, q, 1:4, :, :, chunk(c)], rr.at[way, q, c])
        for d in (1, 3, 2, 0):
            for q in (0, 1):
                for n in range(c * WIDE // NT, (c + 1) * WIDE // NT):
                    cols = slice(n * NT, (n + 1) * NT)
                    rows = jnp.concatenate([ret[way, q, i, d, :, cols] for i in range(SIDE)], axis=0)
                    if way == BWD:
                        total = dot(sel_t[2, q, d], rows)
                    else:
                        total = dot(sel_t[0, q, d], rows) + dot(sel_t[1, q, d], rows)
                    if d == 0:
                        own[way, q, :, cols] = total
                    else:
                        part[way, q, d - 1, :, cols] = total.astype(BF16)
                if d:
                    there = gath.at[way, q, SIDE - d - 1, :, chunk(c)]
                    send(part.at[way, q, d - 1, :, chunk(c)], there, cs.at[way], cr.at[way, q, c], first(q, d))

    def cross(way, c):
        cols = chunk(c)
        for q in (0, 1):
            take(gath.at[way, q, :, :, cols], cr.at[way, q, c])
            total = own[way, q, :, cols]
            for d in range(SIDE - 1):
                total = total + gath[way, q, d, :, cols].astype(F32)
            zout[way, q, :, cols] = total[TOK:].astype(BF16)
            send(zout.at[way, q, :, cols], zin.at[way, q, :, cols], qs.at[way], qr.at[way, q, c], partner)
            own[way, q, :TOK, cols] = total[:TOK]

    def crossed(way, q, c):
        cols = chunk(c)
        take(zin.at[way, q, :, cols], qr.at[way, q, c])
        return own[way, q, :TOK, cols] + zin[way, q, :, cols].astype(F32)

    def end_backward():
        dn = jnp.concatenate([crossed(BWD, q, c) for q in (0, 1) for c in range(CHUNKS)], axis=1)
        xb = xb_ref[...].astype(F32)
        scale = lax.rsqrt(jnp.mean(xb * xb, axis=-1, keepdims=True) + EPS)
        v = gain_ref[...].astype(F32) * dn
        inner = jnp.mean(xb * v, axis=-1, keepdims=True)
        dx = scale * v - xb * (scale * scale * scale) * inner
        last[BWD] = (gr_ref[...].astype(F32) + dx).astype(BF16)
        send(last.at[BWD], outb_ref, ps.at[BWD], pr.at[BWD], behind)

    def end_forward(c):
        for q in (0, 1):
            cols = slice(q * HALF + c * WIDE, q * HALF + (c + 1) * WIDE)
            last[FWD, :, cols] = (xf_ref[:, cols].astype(F32) + crossed(FWD, q, c)).astype(BF16)
            send(last.at[FWD, :, cols], outf_ref.at[:, cols], ps.at[FWD], pr.at[FWD], ahead)

    for c in range(CHUNKS):
        send_back(FWD, c, make_o)
        combine(BWD, c)
    for c in range(CHUNKS):
        cross(BWD, c)
        combine(FWD, c)
    end_backward()
    for c in range(CHUNKS):
        cross(FWD, c)
    for c in range(CHUNKS):
        end_forward(c)

    take(outb_ref, pr.at[BWD])
    take(outf_ref, pr.at[FWD])
    take(meta_z, mz_s)
    take(meta_d.at[:, 1:4], ma_s)
    for t in (G, HB, HF):
        take(dense.at[t, :, 1:4], ds_s.at[t])
        if t == HF:
            take(pool.at[t, :, 1:4], xs.at[t])
        for q in (0, 1):
            take(dense.at[t, q, 0, 0], zs.at[t, q])
    for way in (FWD, BWD):
        for c in range(CHUNKS):
            take(pool.at[way, :, 1:4, :, :, chunk(c)], rs.at[way, c])
        take(part.at[way], cs.at[way])
        take(zout.at[way], qs.at[way])
        take(last.at[way], ps.at[way])


def local(*args):
    args = [a.reshape(a.shape[-2:]) for a in args]
    for k in (1, 2, 5, 6):
        args[k] = args[k].T
    vm = pl.BlockSpec(memory_space=pltpu.VMEM)
    hbm = pl.BlockSpec(memory_space=pl.ANY)
    dma = pltpu.SemaphoreType.DMA
    out = jax.ShapeDtypeStruct((TOK, D), BF16)
    got = pl.pallas_call(
        kernel,
        name="expert_layer",
        out_shape=(out, out),
        in_specs=[vm] * 8 + [hbm] * 3,
        out_specs=(vm, vm),
        scratch_shapes=[
            pltpu.VMEM((D, FF), BF16),
            pltpu.VMEM((D, FF), BF16),
            pltpu.VMEM((FF, D), BF16),
            pltpu.VMEM((3, 2, SIDE, 2, TOK, HALF), BF16),
            pltpu.VMEM((3, 2, SIDE, SIDE, PAIR, HALF), BF16),
            pltpu.VMEM((3, 2, SIDE, SIDE, PAIR, HALF), BF16),
            pltpu.VMEM((2, 2, SIDE, SIDE, PAIR, HALF), BF16),
            pltpu.VMEM((2, 2, SIDE - 1, 2 * TOK, HALF), BF16),
            pltpu.VMEM((2, 2, 2 * TOK, HALF), F32),
            pltpu.VMEM((2, 2, SIDE - 1, 2 * TOK, HALF), BF16),
            pltpu.VMEM((2, 2, TOK, HALF), BF16),
            pltpu.VMEM((2, 2, TOK, HALF), BF16),
            pltpu.VMEM((2, TOK, D), BF16),
            pltpu.VMEM((SIDE * SIDE * PAIR, FF), BF16),
            pltpu.VMEM((SIDE * SIDE * PAIR, FF), BF16),
            pltpu.VMEM((2, 2, SIDE, 8, 128), F32),
            pltpu.VMEM((2, SIDE, 8, 128), F32),
            pltpu.VMEM((2, SIDE, 2, 8, 128), F32),
            pltpu.VMEM((2, 2, SIDE, SIDE * PAIR, 2 * TOK), BF16),
            pltpu.VMEM((3, 2, SIDE, 2 * TOK, SIDE * PAIR), BF16),
            pltpu.VMEM((2, SIDE, SIDE * PAIR, 128), F32),
            dma((3,)),
            dma,
            dma,
            dma,
            dma,
            dma((3, 2)),
            dma((3, 2)),
            dma((3,)),
            dma((3, 2, SIDE, 2)),
            dma((3,)),
            dma((3, 2)),
            dma((2, CHUNKS)),
            dma((2, 2, CHUNKS)),
            dma((2,)),
            dma((2, 2, CHUNKS)),
            dma((2,)),
            dma((2, 2, CHUNKS)),
            dma((2,)),
            dma((2,)),
        ],
        compiler_params=pltpu.CompilerParams(
            collective_id=0, has_side_effects=True, vmem_limit_bytes=62 * 1024 * 1000
        ),
        cost_estimate=pl.CostEstimate(
            flops=2 * 8 * 768 * D * FF, bytes_accessed=3 * 2 * D * FF, transcendentals=2 * 768 * FF
        ),
    )(*args)
    return tuple(o[None] for o in got)


def solution(mesh):
    rows = P("pipe", "ep", None)
    weights = P("pipe", "ep", None, None)
    return jax.shard_map(
        local,
        mesh=mesh,
        in_specs=(rows,) * 7 + (P("pipe", None),) + (weights,) * 3,
        out_specs=(rows, rows),
        check_vma=False,
    )
```

```python
import functools

import jax
import jax.numpy as jnp
from jax import lax
from jax.experimental import pallas as pl
from jax.experimental.pallas import tpu as pltpu
from jax.sharding import PartitionSpec as P

EPS = 1e-06
MESH = pl.DeviceIdType.MESH
F32, BF16 = jnp.float32, jnp.bfloat16

SIDE = 4
TOK = 64
CAP = 24
PAIR = 2 * CAP
D = 2048
HALF = D // 2
CHUNKS = 4
WIDE = HALF // CHUNKS
FF = 768
TOP = 8
NT = 256
G, HB, HF = 0, 1, 2
FWD, BWD = 0, 1


def dot(a, b):
    return jnp.dot(a, b, preferred_element_type=F32)


def dot_t(a, b):
    return lax.dot_general(a, b, (((1,), (1,)), ((), ())), preferred_element_type=F32)


def kernel(
    xf_ref, idf_ref, rtf_ref, xb_ref, gr_ref, idb_ref, rtb_ref, gain_ref, wg_hbm, wu_hbm, wd_hbm,
    outf_ref, outb_ref,
    wg, wu, wd, dense, pool, slots, ret, part, held, via, own, gath, zout, zin, last, act1, act2,
    meta, meta_z, meta_d, sel, sel_t, slot_w,
    w_sem, mz_s, mz_r, ma_s, ma_r, zs, zr, ds_s, ds_r, xs, xr, rs, rr, vr, cs, cr, qs, qr, ps, pr,
):
    p = lax.axis_index("pipe")
    e = lax.axis_index("ep")
    x, y, z = e // 8, lax.rem(e // 2, SIDE), lax.rem(e, 2)

    def at(dx, dy, dz):
        return (p, lax.rem(x + dx, SIDE) * 8 + lax.rem(y + dy, SIDE) * 2 + lax.rem(z + dz, 2))

    def first(q, d):
        return at(0, d, 0) if q == 0 else at(d, 0, 0)

    def second(q, d):
        return first(1 - q, d)

    partner = at(0, 0, 1)
    ahead, behind = (lax.rem(p + 1, 8), e), (lax.rem(p + 7, 8), e)

    def send(src, dst, s, r, device):
        pltpu.make_async_remote_copy(
            src_ref=src, dst_ref=dst, send_sem=s, recv_sem=r, device_id=device, device_id_type=MESH
        ).start()

    def take(ref, sem):
        pltpu.make_async_copy(ref, ref, sem).wait()

    barrier = pltpu.get_barrier_semaphore()
    for device in [partner, ahead, behind] + [first(q, d) for q in (0, 1) for d in (1, 2, 3)]:
        pl.semaphore_signal(barrier, inc=1, device_id=device, device_id_type=MESH)
    loads = [
        pltpu.make_async_copy(src, dst, w_sem.at[i])
        for i, (src, dst) in enumerate(((wg_hbm, wg), (wu_hbm, wu), (wd_hbm, wd)))
    ]
    for load in loads:
        load.start()

    def send_across(t, q):
        send(dense.at[t, q, 0, 0], dense.at[t, q, 0, 1], zs.at[t, q], zr.at[t, q], partner)

    def to_first(t, q, d, dz, to):
        there = dense.at[t, q, (d - to) % SIDE, dz]
        send(dense.at[t, q, d, dz], there, ds_s.at[t], ds_r.at[t, q, (d - to) % SIDE, dz], first(q, to))

    def send_own(t):
        for to in (1, 3):
            for q in (0, 1):
                to_first(t, q, 0, 0, to)

    def forward(t, dz):
        for d, to, cols in ((3, 1, slice(0, HALF // 2)), (1, 3, slice(HALF // 2, HALF))):
            for q in (0, 1):
                take(dense.at[t, q, d, dz], ds_r.at[t, q, d, dz])
                mine = dense.at[t, q, d, dz, :, cols]
                send(mine, dense.at[t, q, 2, dz, :, cols], ds_s.at[t], ds_r.at[t, q, 2, dz], first(q, to))

    def normed(ref, t):
        v = ref[...].astype(F32)
        scale = lax.rsqrt(jnp.mean(v * v, axis=-1, keepdims=True) + EPS)
        h = (v * scale * gain_ref[...].astype(F32)).astype(BF16)
        for q in (0, 1):
            dense[t, q, 0, 0] = h[:, q * HALF : (q + 1) * HALF]

    row = lax.broadcasted_iota(jnp.int32, (128, 128), 0)
    i, d, q, dz = row % 4, (row // 8) % 4, (row // 32) % 2, row // 64
    ex = jnp.where(q == 0, i, d)
    ey = jnp.where(q == 0, d, i)
    expert = ((x + ex) % SIDE) * 8 + ((y + ey) % SIDE) * 2 + (z + dz) % 2
    ids = jnp.concatenate([idf_ref[...], idb_ref[...]], axis=1)
    route = jnp.concatenate([rtf_ref[...], rtb_ref[...]], axis=1)
    route = route / jnp.sum(route, axis=0, keepdims=True)
    picked = jnp.zeros((128, 128), F32)
    weight = jnp.zeros((128, 128), F32)
    for k in range(TOP):
        hit = jnp.broadcast_to(ids[k : k + 1], (128, 128)) == expert
        picked = jnp.where(hit, 1.0, picked)
        weight = jnp.where(hit, jnp.broadcast_to(route[k : k + 1], (128, 128)), weight)
    early = lax.broadcasted_iota(jnp.int32, (128, 128), 0)
    late = lax.broadcasted_iota(jnp.int32, (128, 128), 1)
    order = jnp.where((early < late) & (early // TOK == late // TOK), 1.0, 0.0).astype(BF16)
    before = dot(picked.astype(BF16), order)
    place = jnp.where(picked > 0.0, before, -1000.0)
    kind = (row // 4) % 2
    meta[...] = jnp.where(kind == 0, place, weight).reshape(2, 2, 4, 8, 128)
    for q in (0, 1):
        dense[G, q, 0, 0] = gr_ref[:, q * HALF : (q + 1) * HALF]
    pl.semaphore_wait(barrier, 9)
    send(meta.at[1], meta_z, mz_s, mz_r, partner)
    for q in (0, 1):
        for d in (1, 2, 3):
            send(meta.at[0, q, d], meta_d.at[q, SIDE - d, 0], ma_s, ma_r, first(q, d))
    send_across(G, 0)
    send_across(G, 1)
    send_own(G)
    normed(xb_ref, HB)
    take(meta_z, mz_r)
    for q in (0, 1):
        for d in (1, 2, 3):
            send(meta_z.at[q, d], meta_d.at[q, SIDE - d, 1], ma_s, ma_r, first(q, d))
        meta_d[q, 0, 0] = meta[0, q, 0]
        meta_d[q, 0, 1] = meta_z[q, 0]
    send_own(HB)
    normed(xf_ref, HF)
    send_own(HF)
    forward(G, 0)
    take(meta_d.at[:, 1:4], ma_r)

    lane = lax.broadcasted_iota(jnp.int32, (8, 128), 1)
    slot = lax.broadcasted_iota(jnp.int32, (PAIR, 128), 0).astype(F32)

    @pl.loop(0, 8)
    def _(n):
        q, d = n // 4, lax.rem(n, 4)
        m0, m1 = meta_d[q, d, 0], meta_d[q, d, 1]
        r0, r1 = pltpu.roll(m0, TOK, 1), pltpu.roll(m1, TOK, 1)
        for way, m in ((FWD, jnp.where(lane < TOK, m0, r1)), (BWD, jnp.where(lane < TOK, r0, m1))):
            shifted = m + jnp.where(lane < TOK, 0.0, 1.0 * CAP)
            ones, weighed = [], []
            for i in range(SIDE):
                hit = jnp.broadcast_to(shifted[i : i + 1], (PAIR, 128)) == slot
                ones.append(jnp.where(hit, 1.0, 0.0))
                weighed.append(jnp.where(hit, jnp.broadcast_to(m[4 + i : 5 + i], (PAIR, 128)), 0.0))
            fill = [jnp.zeros((256 - SIDE * PAIR, 128), F32)]
            one = jnp.concatenate(ones, axis=0)
            w = jnp.concatenate(weighed, axis=0)
            sel[way, q, d] = one.astype(BF16)
            if way == BWD:
                sum_w = jnp.sum(w, axis=1, keepdims=True)
                slot_w[q, d] = jnp.broadcast_to(sum_w, (SIDE * PAIR, 128))
                back = jnp.concatenate([one] + fill, axis=0).T
                sel_t[2, q, d] = back[:, : SIDE * PAIR].astype(BF16)
            else:
                back = jnp.concatenate([w] + fill, axis=0).T[:, : SIDE * PAIR]
                high = back.astype(BF16)
                sel_t[0, q, d] = high
                sel_t[1, q, d] = (back - high.astype(F32)).astype(BF16)

    def block(ref, q, a, b):
        return ref.at[a, b] if q == 1 else ref.at[b, a]

    def send_slots(t, d):
        way = FWD if t == HF else BWD
        for q in (0, 1):

            @pl.loop(0, HALF // NT)
            def _(n, q=q):
                cols = pl.ds(pl.multiple_of(n * NT, NT), NT)
                rows = dot(sel[way, q, d], dense[t, q, d, :, :, cols].reshape(2 * TOK, NT))
                if t == G:
                    rows = rows * jnp.concatenate([slot_w[q, d]] * (NT // 128), axis=1)
                rows = rows.astype(BF16)
                block(slots.at[t, q], q, d, 0)[:, cols] = rows[:PAIR]
                for k in range(1, SIDE):
                    pool[t, q, k, d, :, cols] = rows[k * PAIR : (k + 1) * PAIR]

        for i in (2, 1, 3):
            for q in (0, 1):
                there = block(slots.at[t, q], q, d, SIDE - i)
                send(pool.at[t, q, i, d], there, xs.at[t], xr.at[t, q], second(q, i))

    def near(t):
        for q in (0, 1):
            take(dense.at[t, q, 0, 1], zr.at[t, q])
            if t < HF:
                send_across(t + 1, q)
            to_first(t, q, 0, 1, 3)
        for q in (0, 1):
            to_first(t, q, 0, 1, 1)
        send_slots(t, 0)

    def far(t):
        forward(t, 1)
        send_slots(t, 3)
        send_slots(t, 1)
        for q in (0, 1):
            for dz in (0, 1):
                take(dense.at[t, q, 2, dz], ds_r.at[t, q, 2, dz])
        send_slots(t, 2)

    near(G)
    forward(HB, 0)
    forward(HF, 0)
    far(G)
    near(HB)
    far(HB)
    near(HF)
    far(HF)

    for load in loads:
        load.wait()

    def arrived(t):
        for q in (0, 1):
            take(slots.at[t, q, 0:3], xr.at[t, q])

    def rows_of(t, q, h):
        return slots[t, q, pl.ds(2 * h, 2)].reshape(2 * SIDE * PAIR, HALF)

    def gate_up(t, h, n):
        cols = pl.ds(pl.multiple_of(n * NT, NT), NT)
        r0, r1 = rows_of(t, 0, h), rows_of(t, 1, h)
        a = dot(r0, wg[:HALF, cols]) + dot(r1, wg[HALF:, cols])
        u = dot(r0, wu[:HALF, cols]) + dot(r1, wu[HALF:, cols])
        return a, u, cols

    n_rows = 2 * SIDE * PAIR

    def chunk(c):
        return slice(c * WIDE, (c + 1) * WIDE)

    def send_back(way, c, make):
        for q in (0, 1):

            @pl.loop(0, 2 * (WIDE // NT))
            def _(step, q=q):
                h, n = lax.rem(step, 2), step // 2 + c * (WIDE // NT)
                cols = pl.ds(pl.multiple_of(n * NT, NT), NT)
                made = make(q, h, n).astype(BF16)
                for k in range(2 * SIDE):
                    one = made[k * PAIR : (k + 1) * PAIR]
                    if q == 0:
                        pool[way, q, 2 * h + k // SIDE, k % SIDE, :, cols] = one
                    else:
                        pool[way, q, k % SIDE, 2 * h + k // SIDE, :, cols] = one

        for d in range(SIDE):
            for b in (1, 3, 2):
                for q in (0, 1):
                    there = ret.at[way, q, SIDE - b, d, :, chunk(c)]
                    send(pool.at[way, q, b, d, :, chunk(c)], there, rs.at[way, c], rr.at[way, q, c], second(q, b))
        for q in (0, 1):
            ret[way, q, 0, :, :, chunk(c)] = pool[way, q, 0, :, :, chunk(c)]

    arrived(G)
    arrived(HB)

    @pl.loop(0, 6)
    def _(step):
        h, n = step // 3, lax.rem(step, 3)
        a, u, cols = gate_up(HB, h, n)
        r0, r1 = rows_of(G, 0, h), rows_of(G, 1, h)
        dact = dot_t(r0, wd[cols, :HALF]) + dot_t(r1, wd[cols, HALF:])
        sg = jax.nn.sigmoid(a)
        rows = pl.ds(pl.multiple_of(h * n_rows, n_rows), n_rows)
        act1[rows, cols] = (dact * u * sg * (1.0 + a * (1.0 - sg))).astype(BF16)
        act2[rows, cols] = (dact * a * sg).astype(BF16)

    for t in (G, HB):
        take(pool.at[t, :, 1:4], xs.at[t])

    def make_dh(q, h, n):
        rows = pl.ds(pl.multiple_of(q * HALF + n * NT, NT), NT)
        mine = pl.ds(pl.multiple_of(h * n_rows, n_rows), n_rows)
        return dot_t(act1[mine], wg[rows]) + dot_t(act2[mine], wu[rows])

    for c in range(CHUNKS):
        send_back(BWD, c, make_dh)
    arrived(HF)

    @pl.loop(0, 6)
    def _(step):
        h, n = step // 3, lax.rem(step, 3)
        a, u, cols = gate_up(HF, h, n)
        rows = pl.ds(pl.multiple_of(h * n_rows, n_rows), n_rows)
        act1[rows, cols] = (a * jax.nn.sigmoid(a) * u).astype(BF16)

    def make_o(q, h, n):
        cols = pl.ds(pl.multiple_of(q * HALF + n * NT, NT), NT)
        return dot(act1[pl.ds(pl.multiple_of(h * n_rows, n_rows), n_rows)], wd[:, cols])

    def combine(way, c):
        for q in (0, 1):
            take(ret.at[way, q, 1:4, :, :, chunk(c)], rr.at[way, q, c])
        for d in (2, 1, 3, 0):
            for q in (0, 1):
                for n in range(c * WIDE // NT, (c + 1) * WIDE // NT):
                    cols = slice(n * NT, (n + 1) * NT)
                    rows = jnp.concatenate([ret[way, q, i, d, :, cols] for i in range(SIDE)], axis=0)
                    if way == BWD:
                        total = dot(sel_t[2, q, d], rows)
                    else:
                        total = dot(sel_t[0, q, d], rows) + dot(sel_t[1, q, d], rows)
                    if d == 0:
                        own[way, q, :, cols] = total
                    elif d == 1:
                        held[way, q, 0, :, cols] = total[:TOK]
                        part[way, q, 0, TOK:, cols] = total[TOK:].astype(BF16)
                    elif d == 3:
                        held[way, q, 1, :, cols] = total[TOK:]
                        part[way, q, 2, :TOK, cols] = total[:TOK].astype(BF16)
                    else:
                        part[way, q, 1, :, cols] = total.astype(BF16)
            for q in (0, 1):
                if d == 2:
                    for k, to in ((0, 1), (1, 3)):
                        mine = part.at[way, q, 1, k * TOK : (k + 1) * TOK, chunk(c)]
                        send(mine, via.at[way, q, k, :, chunk(c)], cs.at[way], vr.at[way, q, c], first(q, to))
                elif d:
                    to_gath(way, q, c, d, 1 if d == 1 else 0)

    def to_gath(way, q, c, d, k):
        mine = part.at[way, q, d - 1, k * TOK : (k + 1) * TOK, chunk(c)]
        there = gath.at[way, q, d // 2, k * TOK : (k + 1) * TOK, chunk(c)]
        send(mine, there, cs.at[way], cr.at[way, q, c], first(q, d))

    def relay(way, c):
        cols = chunk(c)
        for q in (0, 1):
            take(via.at[way, q, :, :, cols], vr.at[way, q, c])
            for k, d in ((0, 1), (1, 3)):
                total = held[way, q, k, :, cols] + via[way, q, k, :, cols].astype(F32)
                part[way, q, d - 1, k * TOK : (k + 1) * TOK, cols] = total.astype(BF16)
                to_gath(way, q, c, d, k)

    def cross(way, c):
        cols = chunk(c)
        for q in (0, 1):
            take(gath.at[way, q, :, :, cols], cr.at[way, q, c])
            total = own[way, q, :, cols]
            for k in range(2):
                total = total + gath[way, q, k, :, cols].astype(F32)
            zout[way, q, :, cols] = total[TOK:].astype(BF16)
            send(zout.at[way, q, :, cols], zin.at[way, q, :, cols], qs.at[way], qr.at[way, q, c], partner)
            own[way, q, :TOK, cols] = total[:TOK]

    def crossed(way, q, c):
        cols = chunk(c)
        take(zin.at[way, q, :, cols], qr.at[way, q, c])
        return own[way, q, :TOK, cols] + zin[way, q, :, cols].astype(F32)

    def end_backward():
        dn = jnp.concatenate([crossed(BWD, q, c) for q in (0, 1) for c in range(CHUNKS)], axis=1)
        xb = xb_ref[...].astype(F32)
        scale = lax.rsqrt(jnp.mean(xb * xb, axis=-1, keepdims=True) + EPS)
        v = gain_ref[...].astype(F32) * dn
        inner = jnp.mean(xb * v, axis=-1, keepdims=True)
        dx = scale * v - xb * (scale * scale * scale) * inner
        last[BWD] = (gr_ref[...].astype(F32) + dx).astype(BF16)
        send(last.at[BWD], outb_ref, ps.at[BWD], pr.at[BWD], behind)

    def end_forward(c):
        for q in (0, 1):
            cols = slice(q * HALF + c * WIDE, q * HALF + (c + 1) * WIDE)
            last[FWD, :, cols] = (xf_ref[:, cols].astype(F32) + crossed(FWD, q, c)).astype(BF16)
            send(last.at[FWD, :, cols], outf_ref.at[:, cols], ps.at[FWD], pr.at[FWD], ahead)

    for c in range(CHUNKS):
        send_back(FWD, c, make_o)
        combine(BWD, c)
        if c:
            relay(BWD, c - 1)
        if c > 1:
            cross(BWD, c - 2)
    relay(BWD, CHUNKS - 1)
    cross(BWD, CHUNKS - 2)
    for c in range(CHUNKS):
        combine(FWD, c)
        if c == 0:
            cross(BWD, CHUNKS - 1)
        else:
            relay(FWD, c - 1)
        if c > 1:
            cross(FWD, c - 2)
        if c == 2:
            end_backward()
    relay(FWD, CHUNKS - 1)
    cross(FWD, CHUNKS - 2)
    end_forward(0)
    cross(FWD, CHUNKS - 1)
    for c in range(1, CHUNKS):
        end_forward(c)

    take(outb_ref, pr.at[BWD])
    take(outf_ref, pr.at[FWD])
    take(meta_z, mz_s)
    take(meta_d.at[:, 1:4], ma_s)
    for t in (G, HB, HF):
        take(dense.at[t, :, 1:4], ds_s.at[t])
        if t == HF:
            take(pool.at[t, :, 1:4], xs.at[t])
        for q in (0, 1):
            take(dense.at[t, q, 0, 0], zs.at[t, q])
    for way in (FWD, BWD):
        for c in range(CHUNKS):
            take(pool.at[way, :, 1:4, :, :, chunk(c)], rs.at[way, c])
        take(part.at[way], cs.at[way])
        take(zout.at[way], qs.at[way])
        take(last.at[way], ps.at[way])


def settle(f_ref, b_ref, outf_ref, outb_ref):
    outf_ref[...] = f_ref[...]
    outb_ref[...] = b_ref[...]


def local(*args):
    args = [a.reshape(a.shape[-2:]) for a in args]
    for k in (1, 2, 5, 6):
        args[k] = args[k].T
    vm = pl.BlockSpec(memory_space=pltpu.VMEM)
    hbm = pl.BlockSpec(memory_space=pl.ANY)
    dma = pltpu.SemaphoreType.DMA
    out = jax.ShapeDtypeStruct((TOK, D), BF16)
    got = pl.pallas_call(
        kernel,
        name="expert_layer",
        out_shape=(out, out),
        in_specs=[vm] * 8 + [hbm] * 3,
        out_specs=(vm, vm),
        scratch_shapes=[
            pltpu.VMEM((D, FF), BF16),
            pltpu.VMEM((D, FF), BF16),
            pltpu.VMEM((FF, D), BF16),
            pltpu.VMEM((3, 2, SIDE, 2, TOK, HALF), BF16),
            pltpu.VMEM((3, 2, SIDE, SIDE, PAIR, HALF), BF16),
            pltpu.VMEM((3, 2, SIDE, SIDE, PAIR, HALF), BF16),
            pltpu.VMEM((2, 2, SIDE, SIDE, PAIR, HALF), BF16),
            pltpu.VMEM((2, 2, SIDE - 1, 2 * TOK, HALF), BF16),
            pltpu.VMEM((2, 2, 2, TOK, HALF), F32),
            pltpu.VMEM((2, 2, 2, TOK, HALF), BF16),
            pltpu.VMEM((2, 2, 2 * TOK, HALF), F32),
            pltpu.VMEM((2, 2, 2, 2 * TOK, HALF), BF16),
            pltpu.VMEM((2, 2, TOK, HALF), BF16),
            pltpu.VMEM((2, 2, TOK, HALF), BF16),
            pltpu.VMEM((2, TOK, D), BF16),
            pltpu.VMEM((SIDE * SIDE * PAIR, FF), BF16),
            pltpu.VMEM((SIDE * SIDE * PAIR, FF), BF16),
            pltpu.VMEM((2, 2, SIDE, 8, 128), F32),
            pltpu.VMEM((2, SIDE, 8, 128), F32),
            pltpu.VMEM((2, SIDE, 2, 8, 128), F32),
            pltpu.VMEM((2, 2, SIDE, SIDE * PAIR, 2 * TOK), BF16),
            pltpu.VMEM((3, 2, SIDE, 2 * TOK, SIDE * PAIR), BF16),
            pltpu.VMEM((2, SIDE, SIDE * PAIR, 128), F32),
            dma((3,)),
            dma,
            dma,
            dma,
            dma,
            dma((3, 2)),
            dma((3, 2)),
            dma((3,)),
            dma((3, 2, SIDE, 2)),
            dma((3,)),
            dma((3, 2)),
            dma((2, CHUNKS)),
            dma((2, 2, CHUNKS)),
            dma((2, 2, CHUNKS)),
            dma((2,)),
            dma((2, 2, CHUNKS)),
            dma((2,)),
            dma((2, 2, CHUNKS)),
            dma((2,)),
            dma((2,)),
        ],
        compiler_params=pltpu.CompilerParams(
            collective_id=0, has_side_effects=True, vmem_limit_bytes=62 * 1024 * 1000
        ),
        cost_estimate=pl.CostEstimate(
            flops=2 * 8 * 768 * D * FF, bytes_accessed=3 * 2 * D * FF, transcendentals=2 * 768 * FF
        ),
    )(*args)
    got = pl.pallas_call(
        settle, name="settle", out_shape=(out, out), in_specs=[vm] * 2, out_specs=(vm, vm)
    )(*got)
    return tuple(o[None] for o in got)


def solution(mesh):
    rows = P("pipe", "ep", None)
    weights = P("pipe", "ep", None, None)
    return jax.shard_map(
        local,
        mesh=mesh,
        in_specs=(rows,) * 7 + (P("pipe", None),) + (weights,) * 3,
        out_specs=(rows, rows),
        check_vma=False,
    )
```

```python
import functools

import jax
import jax.numpy as jnp
from jax import lax
from jax.experimental import pallas as pl
from jax.experimental.pallas import tpu as pltpu
from jax.sharding import PartitionSpec as P

EPS = 1e-06
MESH = pl.DeviceIdType.MESH
F32, BF16 = jnp.float32, jnp.bfloat16

SIDE = 4
TOK = 64
CAP = 24
PAIR = 2 * CAP
D = 2048
HALF = D // 2
CHUNKS = 4
WIDE = HALF // CHUNKS
FF = 768
TOP = 8
NT = 256
G, HB, HF = 0, 1, 2
FWD, BWD = 0, 1


def dot(a, b):
    return jnp.dot(a, b, preferred_element_type=F32)


def dot_t(a, b):
    return lax.dot_general(a, b, (((1,), (1,)), ((), ())), preferred_element_type=F32)


def kernel(
    xf_ref, idf_ref, rtf_ref, xb_ref, gr_ref, idb_ref, rtb_ref, gain_ref, wg_hbm, wu_hbm, wd_hbm,
    outf_ref, outb_ref,
    wg, wu, wd, dense, pool, slots, ret, part, held, via, own, gath, zout, zin, last, act1, act2,
    meta, meta_z, meta_d, sel, sel_t, slot_w,
    w_sem, mz_s, mz_r, ma_s, ma_r, zs, zr, ds_s, ds_r, xs, xr, rs, rr, vr, cs, cr, qs, qr, ps, pr,
):
    p = lax.axis_index("pipe")
    e = lax.axis_index("ep")
    x, y, z = e // 8, lax.rem(e // 2, SIDE), lax.rem(e, 2)

    def at(dx, dy, dz):
        return (p, lax.rem(x + dx, SIDE) * 8 + lax.rem(y + dy, SIDE) * 2 + lax.rem(z + dz, 2))

    def first(q, d):
        return at(0, d, 0) if q == 0 else at(d, 0, 0)

    def second(q, d):
        return first(1 - q, d)

    partner = at(0, 0, 1)
    ahead, behind = (lax.rem(p + 1, 8), e), (lax.rem(p + 7, 8), e)

    def send(src, dst, s, r, device):
        pltpu.make_async_remote_copy(
            src_ref=src, dst_ref=dst, send_sem=s, recv_sem=r, device_id=device, device_id_type=MESH
        ).start()

    def take(ref, sem):
        pltpu.make_async_copy(ref, ref, sem).wait()

    barrier = pltpu.get_barrier_semaphore()
    for device in [partner, ahead, behind] + [first(q, d) for q in (0, 1) for d in (1, 2, 3)]:
        pl.semaphore_signal(barrier, inc=1, device_id=device, device_id_type=MESH)
    loads = [
        pltpu.make_async_copy(src, dst, w_sem.at[i])
        for i, (src, dst) in enumerate(((wg_hbm, wg), (wu_hbm, wu), (wd_hbm, wd)))
    ]
    for load in loads:
        load.start()

    def send_across(t, q):
        send(dense.at[t, q, 0, 0], dense.at[t, q, 0, 1], zs.at[t, q], zr.at[t, q], partner)

    def to_first(t, q, d, dz, to):
        there = dense.at[t, q, (d - to) % SIDE, dz]
        send(dense.at[t, q, d, dz], there, ds_s.at[t], ds_r.at[t, q, (d - to) % SIDE, dz], first(q, to))

    def send_own(t):
        for to in (1, 3):
            for q in (0, 1):
                to_first(t, q, 0, 0, to)

    def forward(t, dz):
        for d, to, cols in ((3, 1, slice(0, HALF // 2)), (1, 3, slice(HALF // 2, HALF))):
            for q in (0, 1):
                take(dense.at[t, q, d, dz], ds_r.at[t, q, d, dz])
                mine = dense.at[t, q, d, dz, :, cols]
                send(mine, dense.at[t, q, 2, dz, :, cols], ds_s.at[t], ds_r.at[t, q, 2, dz], first(q, to))

    def normed(ref, t):
        v = ref[...].astype(F32)
        scale = lax.rsqrt(jnp.mean(v * v, axis=-1, keepdims=True) + EPS)
        h = (v * scale * gain_ref[...].astype(F32)).astype(BF16)
        for q in (0, 1):
            dense[t, q, 0, 0] = h[:, q * HALF : (q + 1) * HALF]

    row = lax.broadcasted_iota(jnp.int32, (128, 128), 0)
    i, d, q, dz = row % 4, (row // 8) % 4, (row // 32) % 2, row // 64
    ex = jnp.where(q == 0, i, d)
    ey = jnp.where(q == 0, d, i)
    expert = ((x + ex) % SIDE) * 8 + ((y + ey) % SIDE) * 2 + (z + dz) % 2
    ids = jnp.concatenate([idf_ref[...], idb_ref[...]], axis=1)
    route = jnp.concatenate([rtf_ref[...], rtb_ref[...]], axis=1)
    route = route / jnp.sum(route, axis=0, keepdims=True)
    picked = jnp.zeros((128, 128), F32)
    weight = jnp.zeros((128, 128), F32)
    for k in range(TOP):
        hit = jnp.broadcast_to(ids[k : k + 1], (128, 128)) == expert
        picked = jnp.where(hit, 1.0, picked)
        weight = jnp.where(hit, jnp.broadcast_to(route[k : k + 1], (128, 128)), weight)
    early = lax.broadcasted_iota(jnp.int32, (128, 128), 0)
    late = lax.broadcasted_iota(jnp.int32, (128, 128), 1)
    order = jnp.where((early < late) & (early // TOK == late // TOK), 1.0, 0.0).astype(BF16)
    before = dot(picked.astype(BF16), order)
    place = jnp.where(picked > 0.0, before, -1000.0)
    kind = (row // 4) % 2
    meta[...] = jnp.where(kind == 0, place, weight).reshape(2, 2, 4, 8, 128)
    for q in (0, 1):
        dense[G, q, 0, 0] = gr_ref[:, q * HALF : (q + 1) * HALF]
    pl.semaphore_wait(barrier, 9)
    send(meta.at[1], meta_z, mz_s, mz_r, partner)
    for q in (0, 1):
        for d in (1, 2, 3):
            send(meta.at[0, q, d], meta_d.at[q, SIDE - d, 0], ma_s, ma_r, first(q, d))
    send_across(G, 0)
    send_across(G, 1)
    send_own(G)
    normed(xb_ref, HB)
    take(meta_z, mz_r)
    for q in (0, 1):
        for d in (1, 2, 3):
            send(meta_z.at[q, d], meta_d.at[q, SIDE - d, 1], ma_s, ma_r, first(q, d))
        meta_d[q, 0, 0] = meta[0, q, 0]
        meta_d[q, 0, 1] = meta_z[q, 0]
    send_own(HB)
    forward(G, 0)
    normed(xf_ref, HF)
    send_own(HF)
    take(meta_d.at[:, 1:4], ma_r)

    lane = lax.broadcasted_iota(jnp.int32, (8, 128), 1)
    slot = lax.broadcasted_iota(jnp.int32, (PAIR, 128), 0).astype(F32)

    @pl.loop(0, 8)
    def _(n):
        q, d = n // 4, lax.rem(n, 4)
        m0, m1 = meta_d[q, d, 0], meta_d[q, d, 1]
        r0, r1 = pltpu.roll(m0, TOK, 1), pltpu.roll(m1, TOK, 1)
        for way, m in ((FWD, jnp.where(lane < TOK, m0, r1)), (BWD, jnp.where(lane < TOK, r0, m1))):
            shifted = m + jnp.where(lane < TOK, 0.0, 1.0 * CAP)
            ones, weighed = [], []
            for i in range(SIDE):
                hit = jnp.broadcast_to(shifted[i : i + 1], (PAIR, 128)) == slot
                ones.append(jnp.where(hit, 1.0, 0.0))
                weighed.append(jnp.where(hit, jnp.broadcast_to(m[4 + i : 5 + i], (PAIR, 128)), 0.0))
            fill = [jnp.zeros((256 - SIDE * PAIR, 128), F32)]
            one = jnp.concatenate(ones, axis=0)
            w = jnp.concatenate(weighed, axis=0)
            sel[way, q, d] = one.astype(BF16)
            if way == BWD:
                sum_w = jnp.sum(w, axis=1, keepdims=True)
                slot_w[q, d] = jnp.broadcast_to(sum_w, (SIDE * PAIR, 128))
                back = jnp.concatenate([one] + fill, axis=0).T
                sel_t[2, q, d] = back[:, : SIDE * PAIR].astype(BF16)
            else:
                back = jnp.concatenate([w] + fill, axis=0).T[:, : SIDE * PAIR]
                high = back.astype(BF16)
                sel_t[0, q, d] = high
                sel_t[1, q, d] = (back - high.astype(F32)).astype(BF16)

    def block(ref, q, a, b):
        return ref.at[a, b] if q == 1 else ref.at[b, a]

    def send_slots(t, d):
        way = FWD if t == HF else BWD
        for q in (0, 1):

            @pl.loop(0, HALF // NT)
            def _(n, q=q):
                cols = pl.ds(pl.multiple_of(n * NT, NT), NT)
                rows = dot(sel[way, q, d], dense[t, q, d, :, :, cols].reshape(2 * TOK, NT))
                if t == G:
                    rows = rows * jnp.concatenate([slot_w[q, d]] * (NT // 128), axis=1)
                rows = rows.astype(BF16)
                block(slots.at[t, q], q, d, 0)[:, cols] = rows[:PAIR]
                for k in range(1, SIDE):
                    pool[t, q, k, d, :, cols] = rows[k * PAIR : (k + 1) * PAIR]

        for i in (2, 1, 3):
            for q in (0, 1):
                there = block(slots.at[t, q], q, d, SIDE - i)
                send(pool.at[t, q, i, d], there, xs.at[t], xr.at[t, q], second(q, i))

    def near(t):
        for q in (0, 1):
            take(dense.at[t, q, 0, 1], zr.at[t, q])
            if t < HF:
                send_across(t + 1, q)
            to_first(t, q, 0, 1, 3)
        for q in (0, 1):
            to_first(t, q, 0, 1, 1)
        send_slots(t, 0)

    def far(t):
        forward(t, 1)
        send_slots(t, 3)
        send_slots(t, 1)
        for q in (0, 1):
            for dz in (0, 1):
                take(dense.at[t, q, 2, dz], ds_r.at[t, q, 2, dz])
        send_slots(t, 2)

    forward(HB, 0)
    forward(HF, 0)
    near(G)
    far(G)
    near(HB)
    far(HB)
    near(HF)
    far(HF)

    for load in loads:
        load.wait()

    def arrived(t):
        for q in (0, 1):
            take(slots.at[t, q, 0:3], xr.at[t, q])

    def rows_of(t, q, h):
        return slots[t, q, pl.ds(2 * h, 2)].reshape(2 * SIDE * PAIR, HALF)

    def gate_up(t, h, n):
        cols = pl.ds(pl.multiple_of(n * NT, NT), NT)
        r0, r1 = rows_of(t, 0, h), rows_of(t, 1, h)
        a = dot(r0, wg[:HALF, cols]) + dot(r1, wg[HALF:, cols])
        u = dot(r0, wu[:HALF, cols]) + dot(r1, wu[HALF:, cols])
        return a, u, cols

    n_rows = 2 * SIDE * PAIR

    def chunk(c):
        return slice(c * WIDE, (c + 1) * WIDE)

    def send_back(way, c, make):
        for q in (0, 1):

            @pl.loop(0, 2 * (WIDE // NT))
            def _(step, q=q):
                h, n = lax.rem(step, 2), step // 2 + c * (WIDE // NT)
                cols = pl.ds(pl.multiple_of(n * NT, NT), NT)
                made = make(q, h, n).astype(BF16)
                for k in range(2 * SIDE):
                    one = made[k * PAIR : (k + 1) * PAIR]
                    if q == 0:
                        pool[way, q, 2 * h + k // SIDE, k % SIDE, :, cols] = one
                    else:
                        pool[way, q, k % SIDE, 2 * h + k // SIDE, :, cols] = one

        for d in range(SIDE):
            for b in (1, 3, 2):
                for q in (0, 1):
                    there = ret.at[way, q, SIDE - b, d, :, chunk(c)]
                    send(pool.at[way, q, b, d, :, chunk(c)], there, rs.at[way, c], rr.at[way, q, c], second(q, b))
        for q in (0, 1):
            ret[way, q, 0, :, :, chunk(c)] = pool[way, q, 0, :, :, chunk(c)]

    arrived(G)
    arrived(HB)

    @pl.loop(0, 6)
    def _(step):
        h, n = step // 3, lax.rem(step, 3)
        a, u, cols = gate_up(HB, h, n)
        r0, r1 = rows_of(G, 0, h), rows_of(G, 1, h)
        dact = dot_t(r0, wd[cols, :HALF]) + dot_t(r1, wd[cols, HALF:])
        sg = jax.nn.sigmoid(a)
        rows = pl.ds(pl.multiple_of(h * n_rows, n_rows), n_rows)
        act1[rows, cols] = (dact * u * sg * (1.0 + a * (1.0 - sg))).astype(BF16)
        act2[rows, cols] = (dact * a * sg).astype(BF16)

    for t in (G, HB):
        take(pool.at[t, :, 1:4], xs.at[t])

    def make_dh(q, h, n):
        rows = pl.ds(pl.multiple_of(q * HALF + n * NT, NT), NT)
        mine = pl.ds(pl.multiple_of(h * n_rows, n_rows), n_rows)
        return dot_t(act1[mine], wg[rows]) + dot_t(act2[mine], wu[rows])

    for c in range(CHUNKS):
        send_back(BWD, c, make_dh)
    arrived(HF)

    @pl.loop(0, 6)
    def _(step):
        h, n = step // 3, lax.rem(step, 3)
        a, u, cols = gate_up(HF, h, n)
        rows = pl.ds(pl.multiple_of(h * n_rows, n_rows), n_rows)
        act1[rows, cols] = (a * jax.nn.sigmoid(a) * u).astype(BF16)

    def make_o(q, h, n):
        cols = pl.ds(pl.multiple_of(q * HALF + n * NT, NT), NT)
        return dot(act1[pl.ds(pl.multiple_of(h * n_rows, n_rows), n_rows)], wd[:, cols])

    def combine(way, c):
        for q in (0, 1):
            take(ret.at[way, q, 1:4, :, :, chunk(c)], rr.at[way, q, c])
        for d in (2, 1, 3, 0):
            for q in (0, 1):
                for n in range(c * WIDE // NT, (c + 1) * WIDE // NT):
                    cols = slice(n * NT, (n + 1) * NT)
                    rows = jnp.concatenate([ret[way, q, i, d, :, cols] for i in range(SIDE)], axis=0)
                    if way == BWD:
                        total = dot(sel_t[2, q, d], rows)
                    else:
                        total = dot(sel_t[0, q, d], rows) + dot(sel_t[1, q, d], rows)
                    if d == 0:
                        own[way, q, :, cols] = total
                    elif d == 1:
                        held[way, q, 0, :, cols] = total[:TOK]
                        part[way, q, 0, TOK:, cols] = total[TOK:].astype(BF16)
                    elif d == 3:
                        held[way, q, 1, :, cols] = total[TOK:]
                        part[way, q, 2, :TOK, cols] = total[:TOK].astype(BF16)
                    else:
                        part[way, q, 1, :, cols] = total.astype(BF16)
            for q in (0, 1):
                if d == 2:
                    for k, to in ((0, 1), (1, 3)):
                        mine = part.at[way, q, 1, k * TOK : (k + 1) * TOK, chunk(c)]
                        send(mine, via.at[way, q, k, :, chunk(c)], cs.at[way], vr.at[way, q, c], first(q, to))
                elif d:
                    to_gath(way, q, c, d, 1 if d == 1 else 0)

    def to_gath(way, q, c, d, k):
        mine = part.at[way, q, d - 1, k * TOK : (k + 1) * TOK, chunk(c)]
        there = gath.at[way, q, d // 2, k * TOK : (k + 1) * TOK, chunk(c)]
        send(mine, there, cs.at[way], cr.at[way, q, c], first(q, d))

    def relay(way, c):
        cols = chunk(c)
        for q in (0, 1):
            take(via.at[way, q, :, :, cols], vr.at[way, q, c])
            for k, d in ((0, 1), (1, 3)):
                total = held[way, q, k, :, cols] + via[way, q, k, :, cols].astype(F32)
                part[way, q, d - 1, k * TOK : (k + 1) * TOK, cols] = total.astype(BF16)
                to_gath(way, q, c, d, k)

    def cross(way, c):
        cols = chunk(c)
        for q in (0, 1):
            take(gath.at[way, q, :, :, cols], cr.at[way, q, c])
            total = own[way, q, :, cols]
            for k in range(2):
                total = total + gath[way, q, k, :, cols].astype(F32)
            zout[way, q, :, cols] = total[TOK:].astype(BF16)
            send(zout.at[way, q, :, cols], zin.at[way, q, :, cols], qs.at[way], qr.at[way, q, c], partner)
            own[way, q, :TOK, cols] = total[:TOK]

    def crossed(way, q, c):
        cols = chunk(c)
        take(zin.at[way, q, :, cols], qr.at[way, q, c])
        return own[way, q, :TOK, cols] + zin[way, q, :, cols].astype(F32)

    def end_backward():
        dn = jnp.concatenate([crossed(BWD, q, c) for q in (0, 1) for c in range(CHUNKS)], axis=1)
        xb = xb_ref[...].astype(F32)
        scale = lax.rsqrt(jnp.mean(xb * xb, axis=-1, keepdims=True) + EPS)
        v = gain_ref[...].astype(F32) * dn
        inner = jnp.mean(xb * v, axis=-1, keepdims=True)
        dx = scale * v - xb * (scale * scale * scale) * inner
        last[BWD] = (gr_ref[...].astype(F32) + dx).astype(BF16)
        send(last.at[BWD], outb_ref, ps.at[BWD], pr.at[BWD], behind)

    def end_forward(c):
        for q in (0, 1):
            cols = slice(q * HALF + c * WIDE, q * HALF + (c + 1) * WIDE)
            last[FWD, :, cols] = (xf_ref[:, cols].astype(F32) + crossed(FWD, q, c)).astype(BF16)
            send(last.at[FWD, :, cols], outf_ref.at[:, cols], ps.at[FWD], pr.at[FWD], ahead)

    for c in range(CHUNKS):
        send_back(FWD, c, make_o)
        combine(BWD, c)
        if c:
            relay(BWD, c - 1)
        if c > 1:
            cross(BWD, c - 2)
    relay(BWD, CHUNKS - 1)
    cross(BWD, CHUNKS - 2)
    for c in range(CHUNKS):
        combine(FWD, c)
        if c == 0:
            cross(BWD, CHUNKS - 1)
        else:
            relay(FWD, c - 1)
        if c > 1:
            cross(FWD, c - 2)
        if c == 2:
            end_backward()
    relay(FWD, CHUNKS - 1)
    cross(FWD, CHUNKS - 2)
    end_forward(0)
    cross(FWD, CHUNKS - 1)
    for c in range(1, CHUNKS):
        end_forward(c)

    take(outb_ref, pr.at[BWD])
    take(outf_ref, pr.at[FWD])
    take(meta_z, mz_s)
    take(meta_d.at[:, 1:4], ma_s)
    for t in (G, HB, HF):
        take(dense.at[t, :, 1:4], ds_s.at[t])
        if t == HF:
            take(pool.at[t, :, 1:4], xs.at[t])
        for q in (0, 1):
            take(dense.at[t, q, 0, 0], zs.at[t, q])
    for way in (FWD, BWD):
        for c in range(CHUNKS):
            take(pool.at[way, :, 1:4, :, :, chunk(c)], rs.at[way, c])
        take(part.at[way], cs.at[way])
        take(zout.at[way], qs.at[way])
        take(last.at[way], ps.at[way])


def settle(f_ref, b_ref, outf_ref, outb_ref):
    outf_ref[...] = f_ref[...]
    outb_ref[...] = b_ref[...]


def local(*args):
    args = [a.reshape(a.shape[-2:]) for a in args]
    for k in (1, 2, 5, 6):
        args[k] = args[k].T
    vm = pl.BlockSpec(memory_space=pltpu.VMEM)
    hbm = pl.BlockSpec(memory_space=pl.ANY)
    dma = pltpu.SemaphoreType.DMA
    out = jax.ShapeDtypeStruct((TOK, D), BF16)
    got = pl.pallas_call(
        kernel,
        name="expert_layer",
        out_shape=(out, out),
        in_specs=[vm] * 8 + [hbm] * 3,
        out_specs=(vm, vm),
        scratch_shapes=[
            pltpu.VMEM((D, FF), BF16),
            pltpu.VMEM((D, FF), BF16),
            pltpu.VMEM((FF, D), BF16),
            pltpu.VMEM((3, 2, SIDE, 2, TOK, HALF), BF16),
            pltpu.VMEM((3, 2, SIDE, SIDE, PAIR, HALF), BF16),
            pltpu.VMEM((3, 2, SIDE, SIDE, PAIR, HALF), BF16),
            pltpu.VMEM((2, 2, SIDE, SIDE, PAIR, HALF), BF16),
            pltpu.VMEM((2, 2, SIDE - 1, 2 * TOK, HALF), BF16),
            pltpu.VMEM((2, 2, 2, TOK, HALF), F32),
            pltpu.VMEM((2, 2, 2, TOK, HALF), BF16),
            pltpu.VMEM((2, 2, 2 * TOK, HALF), F32),
            pltpu.VMEM((2, 2, 2, 2 * TOK, HALF), BF16),
            pltpu.VMEM((2, 2, TOK, HALF), BF16),
            pltpu.VMEM((2, 2, TOK, HALF), BF16),
            pltpu.VMEM((2, TOK, D), BF16),
            pltpu.VMEM((SIDE * SIDE * PAIR, FF), BF16),
            pltpu.VMEM((SIDE * SIDE * PAIR, FF), BF16),
            pltpu.VMEM((2, 2, SIDE, 8, 128), F32),
            pltpu.VMEM((2, SIDE, 8, 128), F32),
            pltpu.VMEM((2, SIDE, 2, 8, 128), F32),
            pltpu.VMEM((2, 2, SIDE, SIDE * PAIR, 2 * TOK), BF16),
            pltpu.VMEM((3, 2, SIDE, 2 * TOK, SIDE * PAIR), BF16),
            pltpu.VMEM((2, SIDE, SIDE * PAIR, 128), F32),
            dma((3,)),
            dma,
            dma,
            dma,
            dma,
            dma((3, 2)),
            dma((3, 2)),
            dma((3,)),
            dma((3, 2, SIDE, 2)),
            dma((3,)),
            dma((3, 2)),
            dma((2, CHUNKS)),
            dma((2, 2, CHUNKS)),
            dma((2, 2, CHUNKS)),
            dma((2,)),
            dma((2, 2, CHUNKS)),
            dma((2,)),
            dma((2, 2, CHUNKS)),
            dma((2,)),
            dma((2,)),
        ],
        compiler_params=pltpu.CompilerParams(
            collective_id=0, has_side_effects=True, vmem_limit_bytes=62 * 1024 * 1000
        ),
        cost_estimate=pl.CostEstimate(
            flops=2 * 8 * 768 * D * FF, bytes_accessed=3 * 2 * D * FF, transcendentals=2 * 768 * FF
        ),
    )(*args)
    got = pl.pallas_call(
        settle, name="settle", out_shape=(out, out), in_specs=[vm] * 2, out_specs=(vm, vm)
    )(*got)
    return tuple(o[None] for o in got)


def solution(mesh):
    rows = P("pipe", "ep", None)
    weights = P("pipe", "ep", None, None)
    return jax.shard_map(
        local,
        mesh=mesh,
        in_specs=(rows,) * 7 + (P("pipe", None),) + (weights,) * 3,
        out_specs=(rows, rows),
        check_vma=False,
    )
```

```python
import functools

import jax
import jax.numpy as jnp
from jax import lax
from jax.experimental import pallas as pl
from jax.experimental.pallas import tpu as pltpu
from jax.sharding import PartitionSpec as P

EPS = 1e-06
MESH = pl.DeviceIdType.MESH
F32, BF16 = jnp.float32, jnp.bfloat16

SIDE = 4
TOK = 64
CAP = 24
PAIR = 2 * CAP
D = 2048
HALF = D // 2
CHUNKS = 4
WIDE = HALF // CHUNKS
FF = 768
TOP = 8
NT = 256
G, HB, HF = 0, 1, 2
FWD, BWD = 0, 1


def dot(a, b):
    return jnp.dot(a, b, preferred_element_type=F32)


def dot_t(a, b):
    return lax.dot_general(a, b, (((1,), (1,)), ((), ())), preferred_element_type=F32)


def kernel(
    xf_ref, idf_ref, rtf_ref, xb_ref, gr_ref, idb_ref, rtb_ref, gain_ref, wg_hbm, wu_hbm, wd_hbm,
    outf_ref, outb_ref,
    wg, wu, wd, dense, pool, slots, ret, part, held, via, own, gath, zout, zin, last, act1, act2,
    meta, meta_z, meta_d, sel, sel_t, slot_w,
    w_sem, mz_s, mz_r, ma_s, ma_r, zs, zr, ds_s, ds_r, xs, xr, rs, rr, vr, cs, cr, qs, qr, ps, pr,
):
    p = lax.axis_index("pipe")
    e = lax.axis_index("ep")
    x, y, z = e // 8, lax.rem(e // 2, SIDE), lax.rem(e, 2)

    def at(dx, dy, dz):
        return (p, lax.rem(x + dx, SIDE) * 8 + lax.rem(y + dy, SIDE) * 2 + lax.rem(z + dz, 2))

    def first(q, d):
        return at(0, d, 0) if q == 0 else at(d, 0, 0)

    def second(q, d):
        return first(1 - q, d)

    partner = at(0, 0, 1)
    ahead, behind = (lax.rem(p + 1, 8), e), (lax.rem(p + 7, 8), e)

    def send(src, dst, s, r, device):
        pltpu.make_async_remote_copy(
            src_ref=src, dst_ref=dst, send_sem=s, recv_sem=r, device_id=device, device_id_type=MESH
        ).start()

    def take(ref, sem):
        pltpu.make_async_copy(ref, ref, sem).wait()

    barrier = pltpu.get_barrier_semaphore()
    for device in [partner, ahead, behind] + [first(q, d) for q in (0, 1) for d in (1, 2, 3)]:
        pl.semaphore_signal(barrier, inc=1, device_id=device, device_id_type=MESH)
    loads = [
        pltpu.make_async_copy(src, dst, w_sem.at[i])
        for i, (src, dst) in enumerate(((wg_hbm, wg), (wu_hbm, wu), (wd_hbm, wd)))
    ]
    for load in loads:
        load.start()

    def send_across(t, q):
        send(dense.at[t, q, 0, 0], dense.at[t, q, 0, 1], zs.at[t, q], zr.at[t, q], partner)

    def to_first(t, q, d, dz, to):
        there = dense.at[t, q, (d - to) % SIDE, dz]
        send(dense.at[t, q, d, dz], there, ds_s.at[t], ds_r.at[t, q, (d - to) % SIDE, dz], first(q, to))

    def send_own(t):
        for to in (1, 3):
            for q in (0, 1):
                to_first(t, q, 0, 0, to)

    def forward(t, dz):
        for d, to, cols in ((3, 1, slice(0, HALF // 2)), (1, 3, slice(HALF // 2, HALF))):
            for q in (0, 1):
                take(dense.at[t, q, d, dz], ds_r.at[t, q, d, dz])
                mine = dense.at[t, q, d, dz, :, cols]
                send(mine, dense.at[t, q, 2, dz, :, cols], ds_s.at[t], ds_r.at[t, q, 2, dz], first(q, to))

    def normed(ref, t):
        v = ref[...].astype(F32)
        scale = lax.rsqrt(jnp.mean(v * v, axis=-1, keepdims=True) + EPS)
        h = (v * scale * gain_ref[...].astype(F32)).astype(BF16)
        for q in (0, 1):
            dense[t, q, 0, 0] = h[:, q * HALF : (q + 1) * HALF]

    row = lax.broadcasted_iota(jnp.int32, (128, 128), 0)
    i, d, q, dz = row % 4, (row // 8) % 4, (row // 32) % 2, row // 64
    ex = jnp.where(q == 0, i, d)
    ey = jnp.where(q == 0, d, i)
    expert = ((x + ex) % SIDE) * 8 + ((y + ey) % SIDE) * 2 + (z + dz) % 2
    ids = jnp.concatenate([idf_ref[...], idb_ref[...]], axis=1)
    route = jnp.concatenate([rtf_ref[...], rtb_ref[...]], axis=1)
    route = route / jnp.sum(route, axis=0, keepdims=True)
    picked = jnp.zeros((128, 128), F32)
    weight = jnp.zeros((128, 128), F32)
    for k in range(TOP):
        hit = jnp.broadcast_to(ids[k : k + 1], (128, 128)) == expert
        picked = jnp.where(hit, 1.0, picked)
        weight = jnp.where(hit, jnp.broadcast_to(route[k : k + 1], (128, 128)), weight)
    early = lax.broadcasted_iota(jnp.int32, (128, 128), 0)
    late = lax.broadcasted_iota(jnp.int32, (128, 128), 1)
    order = jnp.where((early < late) & (early // TOK == late // TOK), 1.0, 0.0).astype(BF16)
    before = dot(picked.astype(BF16), order)
    place = jnp.where(picked > 0.0, before, -1000.0)
    kind = (row // 4) % 2
    meta[...] = jnp.where(kind == 0, place, weight).reshape(2, 2, 4, 8, 128)
    for q in (0, 1):
        dense[G, q, 0, 0] = gr_ref[:, q * HALF : (q + 1) * HALF]
    pl.semaphore_wait(barrier, 9)
    send(meta.at[1], meta_z, mz_s, mz_r, partner)
    for q in (0, 1):
        for d in (1, 2, 3):
            send(meta.at[0, q, d], meta_d.at[q, SIDE - d, 0], ma_s, ma_r, first(q, d))
    send_across(G, 0)
    send_across(G, 1)
    send_own(G)
    normed(xb_ref, HB)
    take(meta_z, mz_r)
    for q in (0, 1):
        for d in (1, 2, 3):
            send(meta_z.at[q, d], meta_d.at[q, SIDE - d, 1], ma_s, ma_r, first(q, d))
        meta_d[q, 0, 0] = meta[0, q, 0]
        meta_d[q, 0, 1] = meta_z[q, 0]
    send_own(HB)
    normed(xf_ref, HF)
    forward(G, 0)
    send_own(HF)
    forward(HB, 0)
    take(meta_d.at[:, 1:4], ma_r)

    lane = lax.broadcasted_iota(jnp.int32, (8, 128), 1)
    slot = lax.broadcasted_iota(jnp.int32, (PAIR, 128), 0).astype(F32)

    @pl.loop(0, 8)
    def _(n):
        q, d = n // 4, lax.rem(n, 4)
        m0, m1 = meta_d[q, d, 0], meta_d[q, d, 1]
        r0, r1 = pltpu.roll(m0, TOK, 1), pltpu.roll(m1, TOK, 1)
        for way, m in ((FWD, jnp.where(lane < TOK, m0, r1)), (BWD, jnp.where(lane < TOK, r0, m1))):
            shifted = m + jnp.where(lane < TOK, 0.0, 1.0 * CAP)
            ones, weighed = [], []
            for i in range(SIDE):
                hit = jnp.broadcast_to(shifted[i : i + 1], (PAIR, 128)) == slot
                ones.append(jnp.where(hit, 1.0, 0.0))
                weighed.append(jnp.where(hit, jnp.broadcast_to(m[4 + i : 5 + i], (PAIR, 128)), 0.0))
            fill = [jnp.zeros((256 - SIDE * PAIR, 128), F32)]
            one = jnp.concatenate(ones, axis=0)
            w = jnp.concatenate(weighed, axis=0)
            sel[way, q, d] = one.astype(BF16)
            if way == BWD:
                sum_w = jnp.sum(w, axis=1, keepdims=True)
                slot_w[q, d] = jnp.broadcast_to(sum_w, (SIDE * PAIR, 128))
                back = jnp.concatenate([one] + fill, axis=0).T
                sel_t[2, q, d] = back[:, : SIDE * PAIR].astype(BF16)
            else:
                back = jnp.concatenate([w] + fill, axis=0).T[:, : SIDE * PAIR]
                high = back.astype(BF16)
                sel_t[0, q, d] = high
                sel_t[1, q, d] = (back - high.astype(F32)).astype(BF16)

    def block(ref, q, a, b):
        return ref.at[a, b] if q == 1 else ref.at[b, a]

    def send_slots(t, d):
        way = FWD if t == HF else BWD
        for q in (0, 1):

            @pl.loop(0, HALF // NT)
            def _(n, q=q):
                cols = pl.ds(pl.multiple_of(n * NT, NT), NT)
                rows = dot(sel[way, q, d], dense[t, q, d, :, :, cols].reshape(2 * TOK, NT))
                if t == G:
                    rows = rows * jnp.concatenate([slot_w[q, d]] * (NT // 128), axis=1)
                rows = rows.astype(BF16)
                block(slots.at[t, q], q, d, 0)[:, cols] = rows[:PAIR]
                for k in range(1, SIDE):
                    pool[t, q, k, d, :, cols] = rows[k * PAIR : (k + 1) * PAIR]

        for i in (2, 1, 3):
            for q in (0, 1):
                there = block(slots.at[t, q], q, d, SIDE - i)
                send(pool.at[t, q, i, d], there, xs.at[t], xr.at[t, q], second(q, i))

    def near(t):
        for q in (0, 1):
            take(dense.at[t, q, 0, 1], zr.at[t, q])
            if t < HF:
                send_across(t + 1, q)
            to_first(t, q, 0, 1, 3)
        for q in (0, 1):
            to_first(t, q, 0, 1, 1)
        send_slots(t, 0)

    def far(t):
        forward(t, 1)
        send_slots(t, 3)
        send_slots(t, 1)
        for q in (0, 1):
            for dz in (0, 1):
                take(dense.at[t, q, 2, dz], ds_r.at[t, q, 2, dz])
        send_slots(t, 2)

    forward(HF, 0)
    near(G)
    far(G)
    near(HB)
    far(HB)
    near(HF)
    far(HF)

    for load in loads:
        load.wait()

    def arrived(t):
        for q in (0, 1):
            take(slots.at[t, q, 0:3], xr.at[t, q])

    def rows_of(t, q, h):
        return slots[t, q, pl.ds(2 * h, 2)].reshape(2 * SIDE * PAIR, HALF)

    def gate_up(t, h, n):
        cols = pl.ds(pl.multiple_of(n * NT, NT), NT)
        r0, r1 = rows_of(t, 0, h), rows_of(t, 1, h)
        a = dot(r0, wg[:HALF, cols]) + dot(r1, wg[HALF:, cols])
        u = dot(r0, wu[:HALF, cols]) + dot(r1, wu[HALF:, cols])
        return a, u, cols

    n_rows = 2 * SIDE * PAIR

    def chunk(c):
        return slice(c * WIDE, (c + 1) * WIDE)

    def send_back(way, c, make):
        for q in (0, 1):

            @pl.loop(0, 2 * (WIDE // NT))
            def _(step, q=q):
                h, n = lax.rem(step, 2), step // 2 + c * (WIDE // NT)
                cols = pl.ds(pl.multiple_of(n * NT, NT), NT)
                made = make(q, h, n).astype(BF16)
                for k in range(2 * SIDE):
                    one = made[k * PAIR : (k + 1) * PAIR]
                    if q == 0:
                        pool[way, q, 2 * h + k // SIDE, k % SIDE, :, cols] = one
                    else:
                        pool[way, q, k % SIDE, 2 * h + k // SIDE, :, cols] = one

        for d in range(SIDE):
            for b in (1, 3, 2):
                for q in (0, 1):
                    there = ret.at[way, q, SIDE - b, d, :, chunk(c)]
                    send(pool.at[way, q, b, d, :, chunk(c)], there, rs.at[way, c], rr.at[way, q, c], second(q, b))
        for q in (0, 1):
            ret[way, q, 0, :, :, chunk(c)] = pool[way, q, 0, :, :, chunk(c)]

    arrived(G)
    arrived(HB)

    @pl.loop(0, 6)
    def _(step):
        h, n = step // 3, lax.rem(step, 3)
        a, u, cols = gate_up(HB, h, n)
        r0, r1 = rows_of(G, 0, h), rows_of(G, 1, h)
        dact = dot_t(r0, wd[cols, :HALF]) + dot_t(r1, wd[cols, HALF:])
        sg = jax.nn.sigmoid(a)
        rows = pl.ds(pl.multiple_of(h * n_rows, n_rows), n_rows)
        act1[rows, cols] = (dact * u * sg * (1.0 + a * (1.0 - sg))).astype(BF16)
        act2[rows, cols] = (dact * a * sg).astype(BF16)

    for t in (G, HB):
        take(pool.at[t, :, 1:4], xs.at[t])

    def make_dh(q, h, n):
        rows = pl.ds(pl.multiple_of(q * HALF + n * NT, NT), NT)
        mine = pl.ds(pl.multiple_of(h * n_rows, n_rows), n_rows)
        return dot_t(act1[mine], wg[rows]) + dot_t(act2[mine], wu[rows])

    for c in range(CHUNKS):
        send_back(BWD, c, make_dh)
    arrived(HF)

    @pl.loop(0, 6)
    def _(step):
        h, n = step // 3, lax.rem(step, 3)
        a, u, cols = gate_up(HF, h, n)
        rows = pl.ds(pl.multiple_of(h * n_rows, n_rows), n_rows)
        act1[rows, cols] = (a * jax.nn.sigmoid(a) * u).astype(BF16)

    def make_o(q, h, n):
        cols = pl.ds(pl.multiple_of(q * HALF + n * NT, NT), NT)
        return dot(act1[pl.ds(pl.multiple_of(h * n_rows, n_rows), n_rows)], wd[:, cols])

    def combine(way, c):
        for q in (0, 1):
            take(ret.at[way, q, 1:4, :, :, chunk(c)], rr.at[way, q, c])
        for d in (2, 1, 3, 0):
            for q in (0, 1):
                for n in range(c * WIDE // NT, (c + 1) * WIDE // NT):
                    cols = slice(n * NT, (n + 1) * NT)
                    rows = jnp.concatenate([ret[way, q, i, d, :, cols] for i in range(SIDE)], axis=0)
                    if way == BWD:
                        total = dot(sel_t[2, q, d], rows)
                    else:
                        total = dot(sel_t[0, q, d], rows) + dot(sel_t[1, q, d], rows)
                    if d == 0:
                        own[way, q, :, cols] = total
                    elif d == 1:
                        held[way, q, 0, :, cols] = total[:TOK]
                        part[way, q, 0, TOK:, cols] = total[TOK:].astype(BF16)
                    elif d == 3:
                        held[way, q, 1, :, cols] = total[TOK:]
                        part[way, q, 2, :TOK, cols] = total[:TOK].astype(BF16)
                    else:
                        part[way, q, 1, :, cols] = total.astype(BF16)
            for q in (0, 1):
                if d == 2:
                    for k, to in ((0, 1), (1, 3)):
                        mine = part.at[way, q, 1, k * TOK : (k + 1) * TOK, chunk(c)]
                        send(mine, via.at[way, q, k, :, chunk(c)], cs.at[way], vr.at[way, q, c], first(q, to))
                elif d:
                    to_gath(way, q, c, d, 1 if d == 1 else 0)

    def to_gath(way, q, c, d, k):
        mine = part.at[way, q, d - 1, k * TOK : (k + 1) * TOK, chunk(c)]
        there = gath.at[way, q, d // 2, k * TOK : (k + 1) * TOK, chunk(c)]
        send(mine, there, cs.at[way], cr.at[way, q, c], first(q, d))

    def relay(way, c):
        cols = chunk(c)
        for q in (0, 1):
            take(via.at[way, q, :, :, cols], vr.at[way, q, c])
            for k, d in ((0, 1), (1, 3)):
                total = held[way, q, k, :, cols] + via[way, q, k, :, cols].astype(F32)
                part[way, q, d - 1, k * TOK : (k + 1) * TOK, cols] = total.astype(BF16)
                to_gath(way, q, c, d, k)

    def cross(way, c):
        cols = chunk(c)
        for q in (0, 1):
            take(gath.at[way, q, :, :, cols], cr.at[way, q, c])
            total = own[way, q, :, cols]
            for k in range(2):
                total = total + gath[way, q, k, :, cols].astype(F32)
            zout[way, q, :, cols] = total[TOK:].astype(BF16)
            send(zout.at[way, q, :, cols], zin.at[way, q, :, cols], qs.at[way], qr.at[way, q, c], partner)
            own[way, q, :TOK, cols] = total[:TOK]

    def crossed(way, q, c):
        cols = chunk(c)
        take(zin.at[way, q, :, cols], qr.at[way, q, c])
        return own[way, q, :TOK, cols] + zin[way, q, :, cols].astype(F32)

    def end_backward():
        dn = jnp.concatenate([crossed(BWD, q, c) for q in (0, 1) for c in range(CHUNKS)], axis=1)
        xb = xb_ref[...].astype(F32)
        scale = lax.rsqrt(jnp.mean(xb * xb, axis=-1, keepdims=True) + EPS)
        v = gain_ref[...].astype(F32) * dn
        inner = jnp.mean(xb * v, axis=-1, keepdims=True)
        dx = scale * v - xb * (scale * scale * scale) * inner
        last[BWD] = (gr_ref[...].astype(F32) + dx).astype(BF16)
        send(last.at[BWD], outb_ref, ps.at[BWD], pr.at[BWD], behind)

    def end_forward(c):
        for q in (0, 1):
            cols = slice(q * HALF + c * WIDE, q * HALF + (c + 1) * WIDE)
            last[FWD, :, cols] = (xf_ref[:, cols].astype(F32) + crossed(FWD, q, c)).astype(BF16)
            send(last.at[FWD, :, cols], outf_ref.at[:, cols], ps.at[FWD], pr.at[FWD], ahead)

    for c in range(CHUNKS):
        send_back(FWD, c, make_o)
        combine(BWD, c)
        if c:
            relay(BWD, c - 1)
        if c > 1:
            cross(BWD, c - 2)
    relay(BWD, CHUNKS - 1)
    cross(BWD, CHUNKS - 2)
    for c in range(CHUNKS):
        combine(FWD, c)
        if c == 0:
            cross(BWD, CHUNKS - 1)
        else:
            relay(FWD, c - 1)
        if c > 1:
            cross(FWD, c - 2)
        if c == 2:
            end_backward()
    relay(FWD, CHUNKS - 1)
    cross(FWD, CHUNKS - 2)
    end_forward(0)
    cross(FWD, CHUNKS - 1)
    for c in range(1, CHUNKS):
        end_forward(c)

    take(outb_ref, pr.at[BWD])
    take(outf_ref, pr.at[FWD])
    take(meta_z, mz_s)
    take(meta_d.at[:, 1:4], ma_s)
    for t in (G, HB, HF):
        take(dense.at[t, :, 1:4], ds_s.at[t])
        if t == HF:
            take(pool.at[t, :, 1:4], xs.at[t])
        for q in (0, 1):
            take(dense.at[t, q, 0, 0], zs.at[t, q])
    for way in (FWD, BWD):
        for c in range(CHUNKS):
            take(pool.at[way, :, 1:4, :, :, chunk(c)], rs.at[way, c])
        take(part.at[way], cs.at[way])
        take(zout.at[way], qs.at[way])
        take(last.at[way], ps.at[way])


def settle(f_ref, b_ref, outf_ref, outb_ref):
    outf_ref[...] = f_ref[...]
    outb_ref[...] = b_ref[...]


def local(*args):
    args = [a.reshape(a.shape[-2:]) for a in args]
    for k in (1, 2, 5, 6):
        args[k] = args[k].T
    vm = pl.BlockSpec(memory_space=pltpu.VMEM)
    hbm = pl.BlockSpec(memory_space=pl.ANY)
    dma = pltpu.SemaphoreType.DMA
    out = jax.ShapeDtypeStruct((TOK, D), BF16)
    got = pl.pallas_call(
        kernel,
        name="expert_layer",
        out_shape=(out, out),
        in_specs=[vm] * 8 + [hbm] * 3,
        out_specs=(vm, vm),
        scratch_shapes=[
            pltpu.VMEM((D, FF), BF16),
            pltpu.VMEM((D, FF), BF16),
            pltpu.VMEM((FF, D), BF16),
            pltpu.VMEM((3, 2, SIDE, 2, TOK, HALF), BF16),
            pltpu.VMEM((3, 2, SIDE, SIDE, PAIR, HALF), BF16),
            pltpu.VMEM((3, 2, SIDE, SIDE, PAIR, HALF), BF16),
            pltpu.VMEM((2, 2, SIDE, SIDE, PAIR, HALF), BF16),
            pltpu.VMEM((2, 2, SIDE - 1, 2 * TOK, HALF), BF16),
            pltpu.VMEM((2, 2, 2, TOK, HALF), F32),
            pltpu.VMEM((2, 2, 2, TOK, HALF), BF16),
            pltpu.VMEM((2, 2, 2 * TOK, HALF), F32),
            pltpu.VMEM((2, 2, 2, 2 * TOK, HALF), BF16),
            pltpu.VMEM((2, 2, TOK, HALF), BF16),
            pltpu.VMEM((2, 2, TOK, HALF), BF16),
            pltpu.VMEM((2, TOK, D), BF16),
            pltpu.VMEM((SIDE * SIDE * PAIR, FF), BF16),
            pltpu.VMEM((SIDE * SIDE * PAIR, FF), BF16),
            pltpu.VMEM((2, 2, SIDE, 8, 128), F32),
            pltpu.VMEM((2, SIDE, 8, 128), F32),
            pltpu.VMEM((2, SIDE, 2, 8, 128), F32),
            pltpu.VMEM((2, 2, SIDE, SIDE * PAIR, 2 * TOK), BF16),
            pltpu.VMEM((3, 2, SIDE, 2 * TOK, SIDE * PAIR), BF16),
            pltpu.VMEM((2, SIDE, SIDE * PAIR, 128), F32),
            dma((3,)),
            dma,
            dma,
            dma,
            dma,
            dma((3, 2)),
            dma((3, 2)),
            dma((3,)),
            dma((3, 2, SIDE, 2)),
            dma((3,)),
            dma((3, 2)),
            dma((2, CHUNKS)),
            dma((2, 2, CHUNKS)),
            dma((2, 2, CHUNKS)),
            dma((2,)),
            dma((2, 2, CHUNKS)),
            dma((2,)),
            dma((2, 2, CHUNKS)),
            dma((2,)),
            dma((2,)),
        ],
        compiler_params=pltpu.CompilerParams(
            collective_id=0, has_side_effects=True, vmem_limit_bytes=62 * 1024 * 1000
        ),
        cost_estimate=pl.CostEstimate(
            flops=2 * 8 * 768 * D * FF, bytes_accessed=3 * 2 * D * FF, transcendentals=2 * 768 * FF
        ),
    )(*args)
    got = pl.pallas_call(
        settle, name="settle", out_shape=(out, out), in_specs=[vm] * 2, out_specs=(vm, vm)
    )(*got)
    return tuple(o[None] for o in got)


def solution(mesh):
    rows = P("pipe", "ep", None)
    weights = P("pipe", "ep", None, None)
    return jax.shard_map(
        local,
        mesh=mesh,
        in_specs=(rows,) * 7 + (P("pipe", None),) + (weights,) * 3,
        out_specs=(rows, rows),
        check_vma=False,
    )
```
